32 devices in a mesh: frag: 2 (over y), aux: 4 (over z), pair: 4 (over x, core).
Axes of the slice: x: 2, y: 2, z: 4, core: 2. Of those that a mesh axis runs over, the one named last changes fastest.
Arguments:
- half_ints: bfloat16 [2560, 8, 4, 128], P(('frag', 'aux', 'pair')), parts along dimension 0, may hold values from -3.5 to 3.5
- partners: int32 [16, 3], P(('frag', 'aux')), parts along dimension 0, may hold values from 0 to 7, as said below
- domains: int32 [16, 128], P('frag'), parts along dimension 0, may hold values from 0 to 1023
- occ_energy: float32 [16, 4], P('frag'), parts along dimension 0, may hold values from -1 to -0.3
- vir_energy: float32 [2048], P('frag'), parts along dimension 0, may hold values from 0.2 to 1.5
Outputs:
- amplitudes: float32 [16, 3, 512, 512], P(('frag', 'aux'), None, 'pair'), parts along dimension 0
- pair_energy: float32 [16, 3, 4, 4], P(('frag', 'aux')), parts along dimension 0
The draws below stay inside these ranges and needn't reach their ends.
There are 2 independent parts, one for each index of `frag`. The reference program is written for one: setup_inputs(seed, part) draws one part's arguments, and reference() takes and returns one part's arrays. A program takes and returns all parts, laid end to end along the dimension named above; each array names one. Nothing has to cross between parts.
Inputs may be any that keep to these rules, and one draw needn't show every extreme that they name: partners[I, 0] = I; every partner J of block I has |J - I| <= 2, and slot 1 is at distance exactly 2.
All inputs are finite; a program needn't handle non-finite values.
Results may differ from the reference program's by a relative error of at most 0.0003.
Values may be sent and summed in bfloat16 or wider, within the bound.
No kernel may reach another device: no remote copies, remote signals or barrier semaphores. Data moves between devices by JAX's collectives and lax.ppermute only.
A program may use at most 128 MiB of HBM per device.

```python
import jax
import jax.numpy as jnp
from jax import lax

DOM = 128
ORB = 4
NPART = 3
NVIR = 1024
BLK_DEV = 2
NBLK = 8
NAUX = 1280


def draw_partners(key, part):
    key = jax.random.fold_in(key, 11)
    key_sign, key_free = jax.random.split(key)
    blocks = jnp.arange(NBLK, dtype=jnp.int32)[:, None]
    random_signs = jax.random.randint(key_sign, (NBLK, 1), 0, 2).astype(jnp.int32) * 2 - 1
    signs = jnp.where(blocks - BLK_DEV < 0, 1, jnp.where(blocks + BLK_DEV > NBLK - 1, -1, random_signs)).astype(jnp.int32)
    free_offsets = jax.random.randint(key_free, (NBLK, NPART - 2), -BLK_DEV, BLK_DEV + 1).astype(jnp.int32)
    free_target = blocks + free_offsets
    free_target = jnp.where(free_target < 0, -free_target, free_target)
    free_target = jnp.where(free_target > NBLK - 1, 2 * (NBLK - 1) - free_target, free_target)
    target = jnp.concatenate([blocks, blocks + signs * BLK_DEV, free_target], axis=1)
    return target.astype(jnp.int32)


def plant(array, own_key, smallest, largest):
    shape = array.shape
    index_at = [jax.random.randint(jax.random.fold_in(own_key, axis), (), 0, shape[axis]) for axis in range(len(shape))]
    array = array.at[tuple(index_at)].set(smallest)
    longest = shape.index(max(shape))
    index_at[longest] = (index_at[longest] + 1) % shape[longest]
    return array.at[tuple(index_at)].set(largest)


def shard_levels(key, extent, cuts, low, largest):
    level = 1.0
    for axis_at, shards_of in cuts:
        draws = jax.random.uniform(jax.random.fold_in(jax.random.fold_in(key, 6), axis_at), (shards_of,), jnp.float32, low / len(cuts), largest / len(cuts))
        level = level * jnp.repeat(jnp.exp(draws), extent[axis_at] // shards_of).reshape((-1,) + (1,) * (len(extent) - 1 - axis_at))
    return level


def scatter_about(own_key, extent, deviation, reach, cuts=(), kind=jnp.bfloat16):
    loudness = shard_levels(own_key, extent, cuts, -0.22, 0.18) if cuts else 1.0
    drawn = jax.random.normal(own_key, extent, jnp.float32) * deviation * loudness
    return jnp.minimum(jnp.maximum(drawn, -reach), reach).astype(kind)


def setup_inputs(seed: int = 0, part: int = 0) -> dict:
    splits = jax.random.split(jax.random.key(seed), 6)
    part_keys = jax.random.split(jax.random.fold_in(splits[5], part), 6)
    return {
        "half_ints": scatter_about(part_keys[0], (NAUX, NBLK, ORB, DOM), (1.414 * NAUX ** -0.25), 3.5, ((0, 16),)),
        "partners": draw_partners(jax.random.fold_in(jax.random.fold_in(splits[5], part), 71), part),
        "domains": plant(jax.random.randint(part_keys[2], (NBLK, DOM), 0, NVIR), jax.random.fold_in(part_keys[2], 1), 0, NVIR - 1).astype(jnp.int32),
        "occ_energy": jnp.clip(jax.random.uniform(part_keys[3], (NBLK, ORB), jnp.float32, -1.0, -0.3), -1.0, -0.3),
        "vir_energy": jnp.clip(jax.random.uniform(part_keys[4], (NVIR,), jnp.float32, 0.2, 1.5), 0.2, 1.5),
    }


def reference(half_ints, partners, domains, occ_energy, vir_energy):
    row_width = ORB * DOM
    flat_rows = half_ints.reshape(NAUX, NBLK, row_width)

    def energies_of(block):
        occ_part = jnp.take(occ_energy, block, axis=0)
        vir_part = jnp.take(vir_energy, jnp.take(domains, block, axis=0), axis=0)
        return (occ_part[:, None] - vir_part[None, :]).reshape(row_width)

    def one_pair(index):
        block = index // NPART
        slot = index % NPART
        other = partners[block, slot]
        left_rows = jnp.take(flat_rows, block, axis=1)
        right_rows = jnp.take(flat_rows, other, axis=1)
        sums = lax.dot_general(left_rows, right_rows, (((0,), (0,)), ((), ())), preferred_element_type=jnp.float32)
        denominator = energies_of(block)[:, None] + energies_of(other)[None, :]
        amps = sums / denominator
        energy = (sums * amps).reshape(ORB, DOM, ORB, DOM).sum(axis=(1, 3)) / (DOM * DOM)
        return amps, energy

    amps_all, energy_all = lax.map(one_pair, jnp.arange(NBLK * NPART, dtype=jnp.int32))
    return (amps_all.reshape(NBLK, NPART, row_width, row_width), energy_all.reshape(NBLK, NPART, ORB, ORB))
```

```python
import jax
import jax.numpy as jnp
from jax import lax
from jax.experimental import pallas as pl
from jax.experimental.pallas import tpu as pltpu
from jax.sharding import PartitionSpec as P

BF16, F16, F32 = jnp.bfloat16, jnp.float16, jnp.float32
VMEM = pl.BlockSpec(memory_space=pltpu.VMEM)
SMEM = pl.BlockSpec(memory_space=pltpu.SMEM)
PARAMS = pltpu.CompilerParams(vmem_limit_bytes=8 * 2**20)
COST = pl.CostEstimate(flops=20_000_000_000, bytes_accessed=40_000_000, transcendentals=0)
PEAK_ROWS = 16


def shape(*dims, dtype=F32):
    return jax.ShapeDtypeStruct(dims, dtype)


def panel_at(depth, orbital, block):
    return pl.ds((orbital * 2 + block) * depth, depth)


def pack(place, raw, count):
    depth, blocks, orbitals, domain = raw.shape

    def kernel(place_ref, raw_ref, *refs):
        near, sends, wide = refs[:3], refs[3:-1], refs[-1]
        z = place_ref[0]
        wide[...] = raw_ref[...].astype(F32)
        peak = jnp.max(jnp.abs(wide[...]).reshape(-1, PEAK_ROWS, domain), axis=0).astype(BF16)

        def panels(out, first):
            for r in range(2):
                block = jnp.clip(first + r, 0, blocks - 1)
                for i in range(orbitals):
                    rows = pl.ds(block * orbitals + i, depth, stride=blocks * orbitals)
                    out[panel_at(depth, i, r), :] = wide[rows, :].astype(BF16)
            out[2 * orbitals * depth :, :] = peak

        for k, out in enumerate(sends, 1):
            panels(out, 2 * lax.rem(z + k, count))
        for k, out in enumerate(near):
            panels(out, 2 * (z - 1 + k))

    one_set = shape(2 * orbitals * depth + PEAK_ROWS, domain, dtype=BF16)
    return pl.pallas_call(
        kernel,
        out_shape=[one_set] * (count + 2),
        in_specs=[SMEM, VMEM],
        out_specs=[VMEM] * (count + 2),
        scratch_shapes=[pltpu.VMEM((depth * blocks * orbitals, domain), F32)],
        compiler_params=PARAMS,
        cost_estimate=COST,
    )(place, raw.reshape(depth * blocks * orbitals, domain))


def relay(place, own, rows):
    count, domain = len(own), own[0].shape[1]

    def kernel(place_ref, *refs):
        own_refs, outs = refs[:count], refs[count:]
        even = lax.rem(place_ref[0], 2) == 0
        for k in range(count - 1):
            at = slice(k * rows, (k + 1) * rows)
            rise = own_refs[k][:rows]
            fall = own_refs[(count - k) % count][:rows]
            outs[0][at] = jnp.where(even, rise, fall)
            outs[1][at] = jnp.where(even, fall, rise)

    return pl.pallas_call(
        kernel,
        out_shape=[shape((count - 1) * rows, domain, dtype=BF16)] * 2,
        in_specs=[SMEM] + [VMEM] * count,
        out_specs=[VMEM] * 2,
        compiler_params=PARAMS,
        cost_estimate=COST,
    )(place, *own)


def product(left, right):
    return lax.dot_general(left, right, (((0,), (0,)), ((), ())), preferred_element_type=F32)


def left_rows(place_ref, own_refs, depth, r):
    p = place_ref[1]
    x, c = p // 2, lax.rem(p, 2)
    order = (2 * x + c, 2 * (1 - x) + c, 2 * x + 1 - c, 2 * (1 - x) + 1 - c)
    columns = [
        jnp.concatenate([ref[panel_at(depth, i, r), :] for ref in own_refs], axis=0) for i in order
    ]
    return jnp.concatenate(columns, axis=1)


def own_pairs(place, own, orbitals):
    count = len(own)
    domain = own[0].shape[1]
    depth = (own[0].shape[0] - PEAK_ROWS) // (2 * orbitals)
    wide = orbitals * domain

    def kernel(place_ref, *refs):
        own_refs, (mine, other, give, peak) = refs[:count], refs[count:]
        for r in range(2):
            right = jnp.concatenate(
                [
                    jnp.concatenate([ref[panel_at(depth, j, r), :] for ref in own_refs], axis=0)
                    for j in range(orbitals)
                ],
                axis=1,
            )
            sums = product(left_rows(place_ref, own_refs, depth, r), right)
            mine[r] = sums[:domain]
            other[r] = sums[domain : 2 * domain]
            give[0, r] = sums[2 * domain : 3 * domain]
            give[1, r] = sums[3 * domain :]
        top = own_refs[0][-PEAK_ROWS:, :].astype(F32)
        for ref in own_refs[1:]:
            top = jnp.maximum(top, ref[-PEAK_ROWS:, :].astype(F32))
        peak[...] = top

    return pl.pallas_call(
        kernel,
        out_shape=[
            shape(2, domain, wide),
            shape(2, domain, wide),
            shape(2, 2, domain, wide),
            shape(PEAK_ROWS, domain),
        ],
        in_specs=[SMEM] + [VMEM] * count,
        out_specs=[VMEM] * 4,
        compiler_params=PARAMS,
        cost_estimate=COST,
    )(place, *own)


def near_pairs(place, choice, own, here, sides, orbitals):
    count = len(own)
    domain = own[0].shape[1]
    depth = (own[0].shape[0] - PEAK_ROWS) // (2 * orbitals)
    rows, wide = 2 * orbitals * depth, orbitals * domain

    def kernel(place_ref, choice_ref, *refs):
        own_refs, here_refs, side_refs = refs[:count], refs[count : count + 2], refs[count + 2 :][:2]
        outs, picked = refs[count + 4 : -1], refs[-1]
        even = lax.rem(place_ref[0], 2) == 0

        def window_panel(w, k, j, parity):
            if w in (2, 3):
                return own_refs[k][panel_at(depth, j, w - 2), :]
            high = w > 3
            if k == 0:
                return here_refs[high][panel_at(depth, j, w % 2), :]
            at = (count - 1 - k if high else k - 1) * rows + (2 * j + w % 2) * depth
            return side_refs[1 - parity if high else parity][at : at + depth, :]

        def pick(w, parity):
            for k in range(count):
                for j in range(orbitals):
                    picked[k * depth : (k + 1) * depth, j * domain : (j + 1) * domain] = (
                        window_panel(w, k, j, parity)
                    )

        for r in range(2):
            left = left_rows(place_ref, own_refs, depth, r)
            for s in range(2):
                chosen = choice_ref[r, s + 1]
                for w in (r, r + 4) if s == 0 else range(r, r + 5):
                    if w in (2, 3):
                        pl.when(chosen == w)(lambda w=w: pick(w, 0))
                    else:
                        for parity in range(2):
                            match = even if parity else jnp.logical_not(even)
                            pl.when((chosen == w) & match)(
                                lambda w=w, parity=parity: pick(w, parity)
                            )
                sums = product(left, picked[...])
                mine, other, give = outs[3 * s : 3 * s + 3]
                mine[r] = sums[:domain]
                other[r] = sums[domain : 2 * domain]
                give[0, r] = sums[2 * domain : 3 * domain]
                give[1, r] = sums[3 * domain :]

    tiles = [shape(2, domain, wide), shape(2, domain, wide), shape(2, 2, domain, wide)]
    return pl.pallas_call(
        kernel,
        out_shape=tiles * 2,
        in_specs=[SMEM, SMEM] + [VMEM] * (count + 4),
        out_specs=[VMEM] * 6,
        scratch_shapes=[pltpu.VMEM((count * depth, wide), BF16)],
        compiler_params=PARAMS,
        cost_estimate=COST,
    )(place, choice, *own, *here, *sides)


def finish(totals, row_vals, col_vals, slot, before, out):
    blocks, rows, width = totals.shape
    orbitals = width // rows

    def kernel(total_ref, row_ref, col_ref, *refs):
        amp_ref, energy_ref = refs[-2:]
        row = row_ref[0]
        for j in range(orbitals):
            at = slice(j * rows, (j + 1) * rows)
            total = total_ref[0, :, at]
            amp = total / (row + col_ref[0, 0, j : j + 1, :])
            amp_ref[0, 0, :, at] = amp
            energy_ref[0, 0, j : j + 1, :] = jnp.sum(total * amp, axis=0, keepdims=True)

    return pl.pallas_call(
        kernel,
        grid=(blocks,),
        out_shape=[shape(*out), shape(blocks, 1, orbitals, rows)],
        in_specs=[
            pl.BlockSpec((1, rows, width), lambda r: (r, 0, 0)),
            pl.BlockSpec((1, rows, rows), lambda r: (r, 0, 0)),
            pl.BlockSpec((1, 1, orbitals, rows), lambda r: (r, slot, 0, 0)),
        ]
        + [pl.BlockSpec(memory_space=pl.ANY)] * len(before),
        out_specs=[
            pl.BlockSpec((1, 1, rows, width), lambda r: (r, slot, 0, 0)),
            pl.BlockSpec((1, 1, orbitals, rows), lambda r: (r, 0, 0, 0)),
        ],
        input_output_aliases={3: 0} if before else {},
        compiler_params=PARAMS,
        cost_estimate=COST,
    )(totals, row_vals, col_vals, *before)


def energies(place, partners, domains, occ_energy, vir_energy):
    blocks, domain = domains.shape
    orbitals = occ_energy.shape[1]
    here, slots = partners.shape
    tables = vir_energy.shape[0] // domain

    def kernel(place_ref, partners_ref, occ_ref, domains_ref, vir_ref, row_ref, col_ref, picked):
        at = domains_ref[...]
        lane, table = lax.rem(at, domain), lax.div(at, domain)
        vir = jnp.zeros(at.shape, F32)
        for t in range(tables):
            values = jnp.broadcast_to(vir_ref[t : t + 1, :], at.shape)
            vir = jnp.where(table == t, jnp.take_along_axis(values, lane, axis=1), vir)
        picked[...] = vir
        z, p = place_ref[0], place_ref[1]
        for r in range(here):
            block = here * z + r
            value = occ_ref[p, block] - picked[pl.ds(block, 1), :]
            row_ref[r] = jnp.broadcast_to(value, (domain, domain)).T
            for s in range(slots):
                other = partners_ref[r, s]
                value = picked[pl.ds(other, 1), :]
                for j in range(orbitals):
                    col_ref[r, s, j : j + 1, :] = occ_ref[j, other] - value

    return pl.pallas_call(
        kernel,
        out_shape=[shape(here, domain, domain), shape(here, slots, orbitals, domain)],
        in_specs=[SMEM] * 3 + [VMEM] * 2,
        out_specs=[VMEM] * 2,
        scratch_shapes=[pltpu.VMEM((blocks, domain), F32)],
        compiler_params=PARAMS,
    )(place, partners, occ_energy.T, domains, vir_energy.reshape(tables, domain))


def fast(half_ints, partners, domains, occ_energy, vir_energy):
    depth, _, orbitals, domain = half_ints.shape
    count = lax.axis_size("aux")
    z, p = lax.axis_index("aux"), lax.axis_index("pair")
    place = jnp.stack([z, p]).astype(jnp.int32)
    sides = [[], []]
    for i in range(count - 1):
        sides[i % 2] += [(i, i + 1), (i + 1, i)]
    swap = [(i, i ^ 1) for i in range(4)]
    cross = [(i, i ^ 2) for i in range(4)]
    choice = partners - 2 * z + 2

    low_here, own_here, high_here, *sends = pack(place, half_ints, count)
    own = [own_here]
    for k, send in enumerate(sends, 1):
        own.append(lax.ppermute(send, "aux", [(i, (i + k) % count) for i in range(count)]))
    row_vals, col_vals = energies(place, partners, domains, occ_energy, vir_energy)
    messages = relay(place, own, 2 * orbitals * depth)
    near = [lax.ppermute(m, "aux", side) for m, side in zip(messages, sides)]
    place, _ = lax.optimization_barrier((place, messages))
    *sums, peak = own_pairs(place, own, orbitals)

    peak = jnp.maximum(peak, lax.ppermute(peak, "pair", swap))
    top = jnp.maximum(jnp.max(peak), 1e-17)
    exponent = jnp.ceil(jnp.log2(top * top * (2 * count * depth))) - 15
    to_half = jnp.exp2(-exponent)

    def reduce(mine, other, give, more=()):
        got = lax.ppermute(give, "pair", swap)
        half = ((other + got[1]) * to_half).reshape(2 * domain, -1)
        half = jnp.concatenate([half, *more]).astype(F16)
        return mine, got[0], lax.ppermute(half, "pair", cross)

    out = partners.shape + (domain, orbitals * domain)
    parts = [reduce(*sums, [jnp.full((8, orbitals * domain), exponent)])]
    from_half = jnp.exp2(parts[0][2][2 * domain, 0].astype(F32))
    place, _ = lax.optimization_barrier((place, parts[0][2]))
    sums = near_pairs(place, choice, own, (low_here, high_here), near, orbitals)
    parts += [reduce(*sums[:3]), reduce(*sums[3:])]
    amps, energy = [], []
    for slot, (mine, got, across) in enumerate(parts):
        across = across[: 2 * domain].astype(F32).reshape(mine.shape)
        total = mine + got + across * from_half
        *amps, part = finish(total, row_vals, col_vals, slot, amps, out)
        energy.append(part)
    amps = amps[0]
    energy = jnp.concatenate(energy, axis=1).sum(axis=3)
    energy = energy / (domain * domain)
    mask = (jnp.arange(orbitals) == p)[None, None, :, None]
    energy = jnp.where(mask, energy[:, :, None, :], 0.0)
    others = [lax.ppermute(energy, "pair", [(i, i ^ k) for i in range(4)]) for k in (1, 2, 3)]
    return amps, energy + others[0] + others[1] + others[2]


def padded(shard, sides, width):
    for axis, dim in sides:
        size, length = (lax.axis_size(axis), shard.shape[dim])
        up = [(i, (i + 1) % size) for i in range(size - 1)]
        down = [(j, i) for i, j in up]
        last = lax.slice_in_dim(shard, length - width, length, axis=dim)
        first = lax.slice_in_dim(shard, 0, width, axis=dim)
        before = lax.ppermute(last, axis, up)
        after = lax.ppermute(first, axis, down)
        shard = jnp.concatenate([before, shard, after], axis=dim)
    return shard


def general(half_ints, partners, domains, occ_energy, vir_energy):
    blocks_here, slots = partners.shape
    orbitals = half_ints.shape[2]
    domain = half_ints.shape[3]
    row_width = orbitals * domain
    first_block = lax.axis_index("aux") * blocks_here
    owned = lax.all_to_all(half_ints, "aux", split_axis=1, concat_axis=0, tiled=True)
    widened = padded(owned, (("aux", 1),), blocks_here)
    flat_rows = widened.reshape(widened.shape[0], 3 * blocks_here, row_width)
    own_blocks = flat_rows[:, blocks_here : 2 * blocks_here]
    positions = (partners - first_block + blocks_here).reshape(-1)
    partner_rows = jnp.take(flat_rows, positions, axis=1).reshape(
        flat_rows.shape[0], blocks_here, slots, row_width
    )
    partial_terms = jnp.einsum(
        "qlr,qlsc->lsrc", own_blocks, partner_rows, preferred_element_type=jnp.float32
    )
    my_sums = lax.psum_scatter(partial_terms, "pair", scatter_dimension=2, tiled=True)
    row_count = my_sums.shape[2]
    row_start = lax.axis_index("pair") * row_count
    block_ids = first_block + jnp.arange(blocks_here, dtype=jnp.int32)
    row_vals = (
        jnp.take(occ_energy, block_ids, axis=0)[:, :, None]
        - jnp.take(vir_energy, jnp.take(domains, block_ids, axis=0), axis=0)[:, None, :]
    )
    row_vals = lax.dynamic_slice_in_dim(
        row_vals.reshape(blocks_here, row_width), row_start, row_count, 1
    )
    col_vals = (
        jnp.take(occ_energy, partners, axis=0)[:, :, :, None]
        - jnp.take(vir_energy, jnp.take(domains, partners, axis=0), axis=0)[:, :, None, :]
    )
    col_vals = col_vals.reshape(blocks_here, slots, row_width)
    denominator = row_vals[:, None, :, None] + col_vals[:, :, None, :]
    amplitudes = my_sums / denominator
    weighted = (
        (my_sums * amplitudes).reshape(blocks_here, slots, row_count, orbitals, domain).sum(axis=4)
    )
    orbital_of = (row_start + jnp.arange(row_count, dtype=jnp.int32)) // domain
    selector = (orbital_of[:, None] == jnp.arange(orbitals, dtype=jnp.int32)[None, :]).astype(
        jnp.float32
    )
    partial_energy = jnp.einsum(
        "lskj,ki->lsij", weighted, selector, precision=lax.Precision.HIGHEST
    )
    pair_energy = lax.psum(partial_energy, "pair") / (domain * domain)
    return (amplitudes, pair_energy)


def on_device(half_ints, partners, domains, occ_energy, vir_energy):
    _, _, orbitals, domain = half_ints.shape
    fits = partners.shape[0] == 2 and domain == 128 and vir_energy.shape[0] % domain == 0
    fits &= lax.axis_size("pair") == orbitals == 4 and lax.axis_size("aux") % 2 == 0
    step = fast if fits and half_ints.shape[0] % 16 == 0 else general
    return step(half_ints, partners, domains, occ_energy, vir_energy)


def solution(mesh):
    return jax.shard_map(
        on_device,
        mesh=mesh,
        in_specs=(
            P(("frag", "aux", "pair"), None, None, None),
            P(("frag", "aux"), None),
            P("frag", None),
            P("frag", None),
            P("frag"),
        ),
        out_specs=(P(("frag", "aux"), None, "pair", None), P(("frag", "aux"), None, None, None)),
        check_vma=False,
    )
```

```python
import jax
import jax.numpy as jnp
from jax import lax
from jax.experimental import pallas as pl
from jax.experimental.pallas import tpu as pltpu
from jax.sharding import PartitionSpec as P

BF16, F16, F32 = jnp.bfloat16, jnp.float16, jnp.float32
VMEM = pl.BlockSpec(memory_space=pltpu.VMEM)
SMEM = pl.BlockSpec(memory_space=pltpu.SMEM)
ANY = pl.BlockSpec(memory_space=pl.ANY)
PARAMS = pltpu.CompilerParams(vmem_limit_bytes=8 * 2**20)
PEAK_ROWS = 16

def shape(*dims, dtype=F32):
    return jax.ShapeDtypeStruct(dims, dtype)


def call(kernel, name, **options):
    return pl.pallas_call(kernel, compiler_params=PARAMS, name=name, **options)


def after(value, *others):
    return lax.optimization_barrier((value, *others))[0]


def panel_at(depth, orbital, block):
    return pl.ds((orbital * 2 + block) * depth, depth)


def depth_of(one_set, orbitals):
    return (one_set.shape[0] - PEAK_ROWS) // (2 * orbitals)


def pack(raw, count):
    depth, blocks, orbitals, domain = raw.shape
    rows, parts = blocks * orbitals, 4
    part = depth * rows // parts

    def kernel(raw_ref, *refs):
        outs, wide = refs[:count], refs[-1]
        z = lax.axis_index("aux")
        wide[...] = raw_ref[...].astype(F32)
        peak = jnp.max(jnp.abs(wide[...]).reshape(-1, PEAK_ROWS, domain), axis=0)
        for k in range(count):
            out = outs[(k + 1) % count]
            block = 2 * jnp.bitwise_xor(z, (k + 1) % count)
            for r in range(2):
                for i in range(orbitals):
                    at = pl.ds((block + r) * orbitals + i, depth, stride=rows)
                    out[panel_at(depth, i, r), :] = wide[at, :].astype(BF16)
            out[2 * orbitals * depth :, :] = peak.astype(BF16)

    one_set = shape(2 * orbitals * depth + PEAK_ROWS, domain, dtype=BF16)
    return call(
        kernel,
        "pack",
        out_shape=[one_set] * count,
        in_specs=[VMEM],
        out_specs=[VMEM] * count,
        scratch_shapes=[
            pltpu.VMEM((depth * rows, domain), F32),
        ],
    )(raw.reshape(depth * rows, domain))


def relay(own, rows):
    domain = own[0].shape[1]

    def kernel(*refs):
        own_refs, outs = refs[:4], refs[4:]
        for out, partner in zip(outs, (1, 3)):
            for k in (1, 2, 3):
                out[(k - 1) * rows : k * rows] = own_refs[k ^ partner][:rows]

    return call(
        kernel,
        "relay",
        out_shape=[shape(3 * rows, domain, dtype=BF16)] * 2,
        in_specs=[VMEM] * 4,
        out_specs=[VMEM] * 2,
    )(*own)


def product(left, right):
    return lax.dot_general(left, right, (((0,), (0,)), ((), ())), preferred_element_type=F32)


def left_rows(own_refs, depth, r):
    p = lax.axis_index("pair")
    x, c = p // 2, lax.rem(p, 2)
    order = (2 * x + c, 2 * (1 - x) + c, 2 * x + 1 - c, 2 * (1 - x) + 1 - c)
    columns = [
        jnp.concatenate([ref[panel_at(depth, i, r), :] for ref in own_refs], axis=0) for i in order
    ]
    return jnp.concatenate(columns, axis=1)


def store_sums(sums, r, mine, other, give):
    domain = sums.shape[0] // 4
    mine[r] = sums[:domain]
    other[r] = sums[domain : 2 * domain]
    give[0, r] = sums[2 * domain : 3 * domain]
    give[1, r] = sums[3 * domain :]


def sum_shapes(orbitals, domain):
    wide = orbitals * domain
    return [shape(2, domain, wide), shape(2, domain, wide), shape(2, 2, domain, wide)]


def own_pairs(own, orbitals):
    count, domain = len(own), own[0].shape[1]
    depth = depth_of(own[0], orbitals)

    def kernel(*refs):
        own_refs, (mine, other, give, peak) = refs[:count], refs[count:]
        top = own_refs[0][-PEAK_ROWS:, :].astype(F32)
        for ref in own_refs[1:]:
            top = jnp.maximum(top, ref[-PEAK_ROWS:, :].astype(F32))
        peak[...] = top
        for r in range(2):
            right = jnp.concatenate(
                [
                    jnp.concatenate([ref[panel_at(depth, j, r), :] for ref in own_refs], axis=0)
                    for j in range(orbitals)
                ],
                axis=1,
            )
            store_sums(product(left_rows(own_refs, depth, r), right), r, mine, other, give)

    return call(
        kernel,
        "own",
        out_shape=sum_shapes(orbitals, domain) + [shape(PEAK_ROWS, domain)],
        in_specs=[VMEM] * count,
        out_specs=[VMEM] * 4,
    )(*own)


def near_pairs(partners, own, here, sides, orbitals, slot):
    count, domain = len(own), own[0].shape[1]
    depth = depth_of(own[0], orbitals)
    rows = 2 * orbitals * depth

    def kernel(partners_ref, *refs):
        own_refs, here_refs, side_refs = refs[:count], refs[count : count + 2], refs[count + 2 :][:2]
        z = lax.axis_index("aux")
        even = lax.rem(z, 2) == 0

        def panels(w, j):
            from_first = (w > 3) == even
            at = (2 * j + lax.rem(w, 2)) * depth
            found = []
            for k in range(count):
                refs, start = (here_refs, at) if k == 0 else (side_refs, at + (k - 1) * rows)
                rows_at = pl.ds(pl.multiple_of(start, 16), depth)
                panel = jnp.where(from_first, refs[0][rows_at, :], refs[1][rows_at, :])
                if slot > 1:
                    own_at = pl.ds(pl.multiple_of(at, 16), depth)
                    panel = jnp.where((w == 2) | (w == 3), own_refs[k][own_at, :], panel)
                found.append(panel)
            return jnp.concatenate(found, axis=0)

        for r in range(2):
            w = partners_ref[r, slot] - 2 * z + 2
            right = jnp.concatenate([panels(w, j) for j in range(orbitals)], axis=1)
            store_sums(product(left_rows(own_refs, depth, r), right), r, *refs[count + 4 :])

    return call(
        kernel,
        f"near{slot}",
        out_shape=sum_shapes(orbitals, domain),
        in_specs=[SMEM] + [VMEM] * (count + 4),
        out_specs=[VMEM] * 3,
    )(partners, *own, *here, *sides)


def scales(first, second, depth, wide):
    def kernel(first_ref, second_ref, top_ref, down_ref, up_ref):
        top = jnp.maximum(first_ref[...], second_ref[...])
        top_ref[...] = top
        top = jnp.maximum(jnp.max(top, axis=(0, 1), keepdims=True), 1e-17)
        exponent = jnp.ceil(jnp.log2(top * top * depth)) - 15
        exponent = jnp.broadcast_to(exponent, down_ref.shape)
        down_ref[...] = jnp.exp2(-exponent)
        up_ref[...] = jnp.exp2(exponent)

    return call(
        kernel,
        "scales",
        out_shape=[shape(*first.shape), shape(8, wide), shape(8, wide)],
        in_specs=[VMEM] * 2,
        out_specs=[VMEM] * 3,
    )(first, second)


def finish(totals, row_vals, col_vals, slot, before, out):
    blocks, rows, width = totals.shape
    orbitals = width // rows

    def kernel(total_ref, row_ref, col_ref, *refs):
        amp_ref, energy_ref, amp, sems = refs[-4:]
        copies = []
        for r in range(blocks):
            row = row_ref[r]
            for j in range(orbitals):
                at = slice(j * rows, (j + 1) * rows)
                total = total_ref[r, :, at]
                tile = total / (row + col_ref[r, slot, j : j + 1, :])
                amp[r, :, at] = tile
                energy_ref[r, j : j + 1, :] = jnp.sum(total * tile, axis=0, keepdims=True)
            copies.append(pltpu.make_async_copy(amp.at[r], amp_ref.at[r, slot], sems.at[r]))
            copies[-1].start()
        for started in copies:
            started.wait()

    return call(
        kernel,
        "finish",
        out_shape=[shape(*out), shape(blocks, orbitals, rows)],
        in_specs=[VMEM] * 3 + [ANY] * len(before),
        out_specs=[ANY, VMEM],
        input_output_aliases={3: 0} if before else {},
        scratch_shapes=[pltpu.VMEM(totals.shape, F32), pltpu.SemaphoreType.DMA((blocks,))],
    )(totals, row_vals, col_vals, *before)


def share_out(shares):
    blocks, orbitals, domain = shares[0].shape
    slots = len(shares)

    def kernel(*refs):
        out = refs[-1]
        p = lax.axis_index("pair")
        row = lax.broadcasted_iota(jnp.int32, (orbitals, orbitals), 0)
        column = lax.broadcasted_iota(jnp.int32, (orbitals, orbitals), 1)
        for r in range(blocks):
            for s in range(slots):
                total = jnp.zeros((orbitals, orbitals), F32)
                sums = jnp.sum(refs[s][r], axis=1, keepdims=True) * (1.0 / (domain * domain))
                for j in range(orbitals):
                    total = jnp.where((row == p) & (column == j), sums[j : j + 1, :], total)
                out[r, s] = total

    return call(
        kernel,
        "share",
        out_shape=shape(blocks, slots, orbitals, orbitals),
        in_specs=[VMEM] * slots,
        out_specs=VMEM,
    )(*shares)


def last(shares):
    def kernel(*refs):
        refs[4][...] = (refs[0][...] + refs[1][...]) + (refs[2][...] + refs[3][...])

    return call(
        kernel,
        "last",
        out_shape=shape(*shares[0].shape),
        in_specs=[VMEM] * 4,
        out_specs=VMEM,
    )(*shares)


def energies(partners, domains, occ_energy, vir_energy):
    blocks, domain = domains.shape
    orbitals = occ_energy.shape[1]
    here, slots = partners.shape
    tables = vir_energy.shape[0] // domain

    def kernel(partners_ref, occ_ref, domains_ref, vir_ref, row_ref, col_ref, picked):
        at = domains_ref[...]
        lane, table = lax.rem(at, domain), lax.div(at, domain)
        vir = jnp.zeros(at.shape, F32)
        for t in range(tables):
            values = jnp.broadcast_to(vir_ref[t : t + 1, :], at.shape)
            vir = jnp.where(table == t, jnp.take_along_axis(values, lane, axis=1), vir)
        picked[...] = vir
        z, p = lax.axis_index("aux"), lax.axis_index("pair")
        for r in range(here):
            block = here * z + r
            value = occ_ref[p, block] - picked[pl.ds(block, 1), :]
            row_ref[r] = jnp.broadcast_to(value, (domain, domain)).T
            for s in range(slots):
                other = partners_ref[r, s]
                value = picked[pl.ds(other, 1), :]
                for j in range(orbitals):
                    col_ref[r, s, j : j + 1, :] = occ_ref[j, other] - value

    return call(
        kernel,
        "energies",
        out_shape=[shape(here, domain, domain), shape(here, slots, orbitals, domain)],
        in_specs=[SMEM] * 2 + [VMEM] * 2,
        out_specs=[VMEM] * 2,
        scratch_shapes=[pltpu.VMEM((blocks, domain), F32)],
    )(partners, occ_energy.T, domains, vir_energy.reshape(tables, domain))


def fast(half_ints, partners, domains, occ_energy, vir_energy):
    depth, _, orbitals, domain = half_ints.shape
    count = lax.axis_size("aux")
    wide = orbitals * domain
    sides = [[(i, i ^ 4) for i in range(16)], [(i, i ^ (12 if 4 <= i < 12 else 1)) for i in range(16)]]
    swap, cross, both = ([(i, i ^ k) for i in range(4)] for k in (1, 2, 3))

    own_here, *sends = pack(half_ints, count)
    here = [sends[0], sends[2]]
    own = [own_here]
    for k, send in enumerate(sends, 1):
        own.append(lax.ppermute(send, "aux", [(i, i ^ k) for i in range(count)]))
    row_vals, col_vals = energies(partners, domains, occ_energy, vir_energy)
    messages = relay(own, 2 * orbitals * depth)
    near = [lax.ppermute(m, ("aux", "pair"), side) for m, side in zip(messages, sides)]
    own[0] = after(own[0], *messages)

    def reduce(mine, other, give):
        got = lax.ppermute(give, "pair", swap)
        return mine, got[0], ((other + got[1]) * to_half[:1]).astype(F16)

    def cross_over(half):
        return lax.ppermute(half, "pair", cross)

    *sums, peak = own_pairs(own, orbitals)
    peak, to_half, _ = scales(peak, lax.ppermute(peak, "pair", swap), 2 * count * depth, wide)
    peak = lax.ppermute(peak, "pair", cross)
    _, _, from_half = scales(peak, peak, 2 * count * depth, wide)

    parts = [reduce(*sums)]
    across = [cross_over(parts[0][2])]
    here[0] = after(here[0], across[0], from_half, row_vals)
    parts.append(reduce(*near_pairs(partners, own, here, near, orbitals, 1)))
    across.append(cross_over(parts[1][2]))
    here[0] = after(here[0], parts[1][0])
    mine, other, give = near_pairs(partners, own, here, near, orbitals, 2)
    parts.append(reduce(mine, other, after(give, parts[1][2])))
    across.append(cross_over(parts[2][2]))
    amps, shares = [], []
    for slot, (mine, got, _) in enumerate(parts):
        back = after(from_half, shares[-1]) if slot else from_half
        total = mine + got + across[slot].astype(F32) * back[:1]
        *amps, share = finish(total, row_vals, col_vals, slot, amps, partners.shape + (domain, wide))
        shares.append(share)
    share = share_out(shares)
    return amps[0], last([share] + [lax.ppermute(share, "pair", to) for to in (swap, cross, both)])


def padded(shard, sides, width):
    for axis, dim in sides:
        size, length = (lax.axis_size(axis), shard.shape[dim])
        up = [(i, (i + 1) % size) for i in range(size - 1)]
        down = [(j, i) for i, j in up]
        last = lax.slice_in_dim(shard, length - width, length, axis=dim)
        first = lax.slice_in_dim(shard, 0, width, axis=dim)
        before = lax.ppermute(last, axis, up)
        after = lax.ppermute(first, axis, down)
        shard = jnp.concatenate([before, shard, after], axis=dim)
    return shard


def general(half_ints, partners, domains, occ_energy, vir_energy):
    blocks_here, slots = partners.shape
    orbitals = half_ints.shape[2]
    domain = half_ints.shape[3]
    row_width = orbitals * domain
    first_block = lax.axis_index("aux") * blocks_here
    owned = lax.all_to_all(half_ints, "aux", split_axis=1, concat_axis=0, tiled=True)
    widened = padded(owned, (("aux", 1),), blocks_here)
    flat_rows = widened.reshape(widened.shape[0], 3 * blocks_here, row_width)
    own_blocks = flat_rows[:, blocks_here : 2 * blocks_here]
    positions = (partners - first_block + blocks_here).reshape(-1)
    partner_rows = jnp.take(flat_rows, positions, axis=1).reshape(
        flat_rows.shape[0], blocks_here, slots, row_width
    )
    partial_terms = jnp.einsum(
        "qlr,qlsc->lsrc", own_blocks, partner_rows, preferred_element_type=jnp.float32
    )
    my_sums = lax.psum_scatter(partial_terms, "pair", scatter_dimension=2, tiled=True)
    row_count = my_sums.shape[2]
    row_start = lax.axis_index("pair") * row_count
    block_ids = first_block + jnp.arange(blocks_here, dtype=jnp.int32)
    row_vals = (
        jnp.take(occ_energy, block_ids, axis=0)[:, :, None]
        - jnp.take(vir_energy, jnp.take(domains, block_ids, axis=0), axis=0)[:, None, :]
    )
    row_vals = lax.dynamic_slice_in_dim(
        row_vals.reshape(blocks_here, row_width), row_start, row_count, 1
    )
    col_vals = (
        jnp.take(occ_energy, partners, axis=0)[:, :, :, None]
        - jnp.take(vir_energy, jnp.take(domains, partners, axis=0), axis=0)[:, :, None, :]
    )
    col_vals = col_vals.reshape(blocks_here, slots, row_width)
    denominator = row_vals[:, None, :, None] + col_vals[:, :, None, :]
    amplitudes = my_sums / denominator
    weighted = (
        (my_sums * amplitudes).reshape(blocks_here, slots, row_count, orbitals, domain).sum(axis=4)
    )
    orbital_of = (row_start + jnp.arange(row_count, dtype=jnp.int32)) // domain
    selector = (orbital_of[:, None] == jnp.arange(orbitals, dtype=jnp.int32)[None, :]).astype(
        jnp.float32
    )
    partial_energy = jnp.einsum(
        "lskj,ki->lsij", weighted, selector, precision=lax.Precision.HIGHEST
    )
    pair_energy = lax.psum(partial_energy, "pair") / (domain * domain)
    return (amplitudes, pair_energy)


def on_device(half_ints, partners, domains, occ_energy, vir_energy):
    _, _, orbitals, domain = half_ints.shape
    fits = partners.shape[0] == 2 and domain == 128 and vir_energy.shape[0] % domain == 0
    fits &= lax.axis_size("pair") == lax.axis_size("aux") == orbitals == 4
    step = fast if fits and half_ints.shape[0] % 16 == 0 else general
    return step(half_ints, partners, domains, occ_energy, vir_energy)


def solution(mesh):
    return jax.shard_map(
        on_device,
        mesh=mesh,
        in_specs=(
            P(("frag", "aux", "pair"), None, None, None),
            P(("frag", "aux"), None),
            P("frag", None),
            P("frag", None),
            P("frag"),
        ),
        out_specs=(P(("frag", "aux"), None, "pair", None), P(("frag", "aux"), None, None, None)),
        check_vma=False,
    )
```

```python
import jax
import jax.numpy as jnp
from jax import lax
from jax.experimental import pallas as pl
from jax.experimental.pallas import tpu as pltpu
from jax.sharding import PartitionSpec as P

BF16, F16, F32 = jnp.bfloat16, jnp.float16, jnp.float32
VMEM = pl.BlockSpec(memory_space=pltpu.VMEM)
SMEM = pl.BlockSpec(memory_space=pltpu.SMEM)
ANY = pl.BlockSpec(memory_space=pl.ANY)
PARAMS = pltpu.CompilerParams(vmem_limit_bytes=8 * 2**20)
PEAK_ROWS = 16
GROUPS = ([[(0, 1)]], [[(1, 1), (0, 2), (1, 2)]])

def shape(*dims, dtype=F32):
    return jax.ShapeDtypeStruct(dims, dtype)


def call(kernel, name, **options):
    return pl.pallas_call(kernel, compiler_params=PARAMS, name=name, **options)


def after(value, *others):
    return lax.optimization_barrier((value, *others))[0]


def panel_at(depth, orbital, block):
    return pl.ds((orbital * 2 + block) * depth, depth)


def depth_of(one_set, orbitals):
    return (one_set.shape[0] - PEAK_ROWS) // (2 * orbitals)


def pack(raw, count):
    depth, blocks, orbitals, domain = raw.shape
    rows, parts = blocks * orbitals, 4
    part = depth * rows // parts

    def kernel(raw_ref, *refs):
        outs, wide = refs[:count], refs[-1]
        z = lax.axis_index("aux")
        wide[...] = raw_ref[...].astype(F32)
        peak = jnp.max(jnp.abs(wide[...]).reshape(-1, PEAK_ROWS, domain), axis=0)
        for k in range(count):
            out = outs[(k + 1) % count]
            block = 2 * jnp.bitwise_xor(z, (k + 1) % count)
            for r in range(2):
                for i in range(orbitals):
                    at = pl.ds((block + r) * orbitals + i, depth, stride=rows)
                    out[panel_at(depth, i, r), :] = wide[at, :].astype(BF16)
            out[2 * orbitals * depth :, :] = peak.astype(BF16)

    one_set = shape(2 * orbitals * depth + PEAK_ROWS, domain, dtype=BF16)
    return call(
        kernel,
        "pack",
        out_shape=[one_set] * count,
        in_specs=[VMEM],
        out_specs=[VMEM] * count,
        scratch_shapes=[
            pltpu.VMEM((depth * rows, domain), F32),
        ],
    )(raw.reshape(depth * rows, domain))


def relay(own, rows):
    domain = own[0].shape[1]

    def kernel(*refs):
        own_refs, outs = refs[:4], refs[4:]
        for out, partner in zip(outs, (1, 3)):
            for k in (1, 2, 3):
                out[(k - 1) * rows : k * rows] = own_refs[k ^ partner][:rows]

    return call(
        kernel,
        "relay",
        out_shape=[shape(3 * rows, domain, dtype=BF16)] * 2,
        in_specs=[VMEM] * 4,
        out_specs=[VMEM] * 2,
    )(*own)


def product(left, right):
    return lax.dot_general(left, right, (((0,), (0,)), ((), ())), preferred_element_type=F32)


def left_rows(own_refs, depth, r):
    p = lax.axis_index("pair")
    x, c = p // 2, lax.rem(p, 2)
    order = (2 * x + c, 2 * (1 - x) + c, 2 * x + 1 - c, 2 * (1 - x) + 1 - c)
    columns = [
        jnp.concatenate([ref[panel_at(depth, i, r), :] for ref in own_refs], axis=0) for i in order
    ]
    return jnp.concatenate(columns, axis=1)


def store_sums(sums, at, mine, other, give):
    domain = sums.shape[0] // 4
    mine[at] = sums[:domain]
    other[at] = sums[domain : 2 * domain]
    give[0, at] = sums[2 * domain : 3 * domain]
    give[1, at] = sums[3 * domain :]


def own_pairs(own, orbitals):
    count, domain = len(own), own[0].shape[1]
    depth = depth_of(own[0], orbitals)
    wide = orbitals * domain

    def kernel(*refs):
        own_refs, (mine, other, give, peak) = refs[:count], refs[count:]
        top = own_refs[0][-PEAK_ROWS:, :].astype(F32)
        for ref in own_refs[1:]:
            top = jnp.maximum(top, ref[-PEAK_ROWS:, :].astype(F32))
        top = jnp.maximum(top[:8], top[8:])
        peak[...] = jnp.concatenate([top] * orbitals, axis=1)
        for n in range(2):
            give[n, 2 * domain :] = peak[...]
        for r in range(2):
            right = jnp.concatenate(
                [
                    jnp.concatenate([ref[panel_at(depth, j, r), :] for ref in own_refs], axis=0)
                    for j in range(orbitals)
                ],
                axis=1,
            )
            at = slice(r * domain, (r + 1) * domain)
            store_sums(product(left_rows(own_refs, depth, r), right), at, mine, other, give)

    return call(
        kernel,
        "own",
        out_shape=[
            shape(2 * domain, wide),
            shape(2 * domain, wide),
            shape(2, 2 * domain + 8, wide),
            shape(8, wide),
        ],
        in_specs=[VMEM] * count,
        out_specs=[VMEM] * 4,
    )(*own)


def near_pairs(partners, own, here, sides, orbitals, groups):
    count, domain = len(own), own[0].shape[1]
    depth = depth_of(own[0], orbitals)
    rows, wide = 2 * orbitals * depth, orbitals * domain

    def kernel(partners_ref, *refs):
        own_refs, here_refs, side_refs = refs[:count], refs[count : count + 2], refs[count + 2 :][:2]
        z = lax.axis_index("aux")
        even = lax.rem(z, 2) == 0

        def panels(w, j, slot):
            from_first = (w > 3) == even
            at = (2 * j + lax.rem(w, 2)) * depth
            found = []
            for k in range(count):
                refs, start = (here_refs, at) if k == 0 else (side_refs, at + (k - 1) * rows)
                rows_at = pl.ds(pl.multiple_of(start, 16), depth)
                panel = jnp.where(from_first, refs[0][rows_at, :], refs[1][rows_at, :])
                if slot > 1:
                    own_at = pl.ds(pl.multiple_of(at, 16), depth)
                    panel = jnp.where((w == 2) | (w == 3), own_refs[k][own_at, :], panel)
                found.append(panel)
            return jnp.concatenate(found, axis=0)

        for n, tiles in enumerate(groups):
            for t, (r, slot) in enumerate(tiles):
                w = partners_ref[r, slot] - 2 * z + 2
                right = jnp.concatenate([panels(w, j, slot) for j in range(orbitals)], axis=1)
                sums = product(left_rows(own_refs, depth, r), right)
                at = slice(t * domain, (t + 1) * domain)
                store_sums(sums, at, *refs[count + 4 + 3 * n :][:3])

    outs = []
    for tiles in groups:
        height = len(tiles) * domain
        outs += [shape(height, wide), shape(height, wide), shape(2, height, wide)]
    return call(
        kernel,
        "near",
        out_shape=outs,
        in_specs=[SMEM] + [VMEM] * (count + 4),
        out_specs=[VMEM] * len(outs),
    )(partners, *own, *here, *sides)


def scale_down(peak, got, depth):
    def kernel(peak_ref, got_ref, top_ref, down_ref):
        top = jnp.maximum(peak_ref[...], got_ref[0, -8:])
        top_ref[...] = top
        top = jnp.maximum(jnp.max(top[:, :128], axis=(0, 1), keepdims=True), 1e-17)
        down_ref[...] = jnp.broadcast_to(32768.0 / (top * top * depth), down_ref.shape)

    return call(
        kernel,
        "scale_down",
        out_shape=[shape(*peak.shape)] * 2,
        in_specs=[VMEM] * 2,
        out_specs=[VMEM] * 2,
    )(peak, got)


def scale_up(top, depth):
    def kernel(top_ref, up_ref):
        top = jnp.maximum(jnp.max(top_ref[:, :128], axis=(0, 1), keepdims=True), 1e-17)
        up_ref[...] = jnp.broadcast_to((top * top * depth) * (1.0 / 32768.0), up_ref.shape)

    return call(
        kernel, "scale_up", out_shape=shape(*top.shape), in_specs=[VMEM], out_specs=VMEM
    )(top)


def amplitude_tiles(total_ref, row_ref, col_ref, amp, energy_ref, tiles, done):
    rows, wide = amp.shape[1:]
    for t, (r, slot) in enumerate(tiles):
        row = row_ref[r]
        for j in range(wide // rows):
            at = slice(j * rows, (j + 1) * rows)
            total = total_ref[t * rows : (t + 1) * rows, at]
            tile = total / (row + col_ref[r, slot, j : j + 1, :])
            amp[t, :, at] = tile
            energy_ref[t, j : j + 1, :] = jnp.sum(total * tile, axis=0, keepdims=True)
        done(t)


def finish(totals, row_vals, col_vals, tiles, before, out):
    rows, wide = out[2:]
    count = len(tiles)

    def kernel(total_ref, row_ref, col_ref, *refs):
        amp_ref, energy_ref, amp, sems = refs[-4:]
        copies = []

        def done(t):
            r, slot = tiles[t]
            copies.append(pltpu.make_async_copy(amp.at[t], amp_ref.at[r, slot], sems.at[t]))
            copies[-1].start()

        amplitude_tiles(total_ref, row_ref, col_ref, amp, energy_ref, tiles, done)
        for started in copies:
            started.wait()

    return call(
        kernel,
        "finish",
        out_shape=[shape(*out), shape(count, wide // rows, rows)],
        in_specs=[VMEM] * 3 + [ANY] * len(before),
        out_specs=[ANY, VMEM],
        input_output_aliases={3: 0} if before else {},
        scratch_shapes=[pltpu.VMEM((count, rows, wide), F32), pltpu.SemaphoreType.DMA((count,))],
    )(totals, row_vals, col_vals, *before)


def finish_last(totals, row_vals, col_vals, tiles, before, shares):
    orbitals, domain = col_vals.shape[2:]
    wide = orbitals * domain
    blocks, slots = col_vals.shape[:2]
    count = len(tiles)
    known = len(shares)

    def kernel(total_ref, row_ref, col_ref, *refs):
        share_refs, (amp_ref, out, energy) = refs[:known], refs[known:]
        amplitude_tiles(total_ref, row_ref, col_ref, amp_ref, energy, tiles, lambda t: None)
        p = lax.axis_index("pair")
        row = lax.broadcasted_iota(jnp.int32, (orbitals, orbitals), 0)
        column = lax.broadcasted_iota(jnp.int32, (orbitals, orbitals), 1)
        for ref, places in zip((*share_refs, energy), (*before, tiles)):
            for t, (r, slot) in enumerate(places):
                sums = jnp.sum(ref[t], axis=1, keepdims=True) * (1.0 / (domain * domain))
                value = jnp.zeros((orbitals, orbitals), F32)
                for j in range(orbitals):
                    value = jnp.where((row == p) & (column == j), sums[j : j + 1, :], value)
                out[r, slot] = value

    return call(
        kernel,
        "finish_last",
        out_shape=[shape(count, domain, wide), shape(blocks, slots, orbitals, orbitals)],
        in_specs=[VMEM] * (3 + known),
        out_specs=[VMEM] * 2,
        scratch_shapes=[pltpu.VMEM((count, orbitals, domain), F32)],
    )(totals, row_vals, col_vals, *shares)


def put(tiles_at, values, amps):
    def kernel(values_ref, _, amp_ref, sems):
        copies = []
        for t, (r, slot) in enumerate(tiles_at):
            copies.append(pltpu.make_async_copy(values_ref.at[t], amp_ref.at[r, slot], sems.at[t]))
            copies[-1].start()
        for started in copies:
            started.wait()

    return call(
        kernel,
        "put",
        out_shape=shape(*amps.shape),
        in_specs=[VMEM, ANY],
        out_specs=ANY,
        input_output_aliases={1: 0},
        scratch_shapes=[pltpu.SemaphoreType.DMA((len(tiles_at),))],
    )(values, amps)


def last(shares):
    def kernel(*refs):
        refs[4][...] = (refs[0][...] + refs[1][...]) + (refs[2][...] + refs[3][...])

    return call(
        kernel,
        "last",
        out_shape=shape(*shares[0].shape),
        in_specs=[VMEM] * 4,
        out_specs=VMEM,
    )(*shares)


def energies(partners, domains, occ_energy, vir_energy):
    blocks, domain = domains.shape
    orbitals = occ_energy.shape[1]
    here, slots = partners.shape
    tables = vir_energy.shape[0] // domain

    def kernel(partners_ref, occ_ref, domains_ref, vir_ref, row_ref, col_ref, picked):
        at = domains_ref[...]
        lane, table = lax.rem(at, domain), lax.div(at, domain)
        vir = jnp.zeros(at.shape, F32)
        for t in range(tables):
            values = jnp.broadcast_to(vir_ref[t : t + 1, :], at.shape)
            vir = jnp.where(table == t, jnp.take_along_axis(values, lane, axis=1), vir)
        picked[...] = vir
        z, p = lax.axis_index("aux"), lax.axis_index("pair")
        for r in range(here):
            block = here * z + r
            value = occ_ref[p, block] - picked[pl.ds(block, 1), :]
            row_ref[r] = jnp.broadcast_to(value, (domain, domain)).T
            for s in range(slots):
                other = partners_ref[r, s]
                value = picked[pl.ds(other, 1), :]
                for j in range(orbitals):
                    col_ref[r, s, j : j + 1, :] = occ_ref[j, other] - value

    return call(
        kernel,
        "energies",
        out_shape=[shape(here, domain, domain), shape(here, slots, orbitals, domain)],
        in_specs=[SMEM] * 2 + [VMEM] * 2,
        out_specs=[VMEM] * 2,
        scratch_shapes=[pltpu.VMEM((blocks, domain), F32)],
    )(partners, occ_energy.T, domains, vir_energy.reshape(tables, domain))


def fast(half_ints, partners, domains, occ_energy, vir_energy):
    depth, _, orbitals, domain = half_ints.shape
    count = lax.axis_size("aux")
    wide = orbitals * domain
    sides = [[(i, i ^ 4) for i in range(16)], [(i, i ^ (12 if 4 <= i < 12 else 1)) for i in range(16)]]
    swap, cross, both = ([(i, i ^ k) for i in range(4)] for k in (1, 2, 3))

    own_here, *sends = pack(half_ints, count)
    here = [sends[0], sends[2]]
    own = [own_here]
    for k, send in enumerate(sends, 1):
        own.append(lax.ppermute(send, "aux", [(i, i ^ k) for i in range(count)]))
    row_vals, col_vals = energies(partners, domains, occ_energy, vir_energy)
    messages = relay(own, 2 * orbitals * depth)
    near = [lax.ppermute(m, ("aux", "pair"), side) for m, side in zip(messages, sides)]
    own[0] = after(own[0], *messages)

    def across_cores(mine, other, give):
        got = lax.ppermute(give, "pair", swap)
        height = mine.shape[0]
        return mine, got, other + got[1, :height]

    def across_chips(other):
        return lax.ppermute((other * to_half[:1]).astype(F16), "pair", cross)

    *sums, peak = own_pairs(own, orbitals)
    mine, got, other = across_cores(*sums)
    top, to_half = scale_down(peak, got, 2 * count * depth)
    parts = [(mine, got, across_chips(other))]
    from_half = scale_up(lax.ppermute(top, "pair", cross), 2 * count * depth)
    here[0] = after(here[0], parts[0][2], from_half, row_vals)

    groups = [[(0, 0), (1, 0)], *GROUPS[0], *GROUPS[1]]
    sums = near_pairs(partners, own, here, near, orbitals, GROUPS[0])
    here[0] = after(here[0], sums[0])
    sums += near_pairs(partners, own, here, near, orbitals, GROUPS[1])
    for n in range(0, len(sums), 3):
        mine, other, give = sums[n : n + 3]
        if n:
            give = after(give, half)
        mine, got, other = across_cores(mine, other, give)
        half = (other * to_half[:1]).astype(F16)
        parts.append((mine, got, lax.ppermute(half, "pair", cross)))

    out = partners.shape + (domain, wide)
    amps, shares = [], []
    for at, (mine, got, across) in enumerate(parts):
        back = after(from_half, shares[-1]) if at else from_half
        total = mine + got[0, : mine.shape[0]] + across.astype(F32) * back[:1]
        if at < len(parts) - 1:
            *amps, share = finish(total, row_vals, col_vals, groups[at], amps, out)
            shares.append(share)
    values, share = finish_last(total, row_vals, col_vals, groups[-1], groups[:-1], shares)
    others = [lax.ppermute(share, "pair", to) for to in (swap, cross, both)]
    return put(groups[-1], values, amps[0]), last([share, *others])


def padded(shard, sides, width):
    for axis, dim in sides:
        size, length = (lax.axis_size(axis), shard.shape[dim])
        up = [(i, (i + 1) % size) for i in range(size - 1)]
        down = [(j, i) for i, j in up]
        last = lax.slice_in_dim(shard, length - width, length, axis=dim)
        first = lax.slice_in_dim(shard, 0, width, axis=dim)
        before = lax.ppermute(last, axis, up)
        after = lax.ppermute(first, axis, down)
        shard = jnp.concatenate([before, shard, after], axis=dim)
    return shard


def general(half_ints, partners, domains, occ_energy, vir_energy):
    blocks_here, slots = partners.shape
    orbitals = half_ints.shape[2]
    domain = half_ints.shape[3]
    row_width = orbitals * domain
    first_block = lax.axis_index("aux") * blocks_here
    owned = lax.all_to_all(half_ints, "aux", split_axis=1, concat_axis=0, tiled=True)
    widened = padded(owned, (("aux", 1),), blocks_here)
    flat_rows = widened.reshape(widened.shape[0], 3 * blocks_here, row_width)
    own_blocks = flat_rows[:, blocks_here : 2 * blocks_here]
    positions = (partners - first_block + blocks_here).reshape(-1)
    partner_rows = jnp.take(flat_rows, positions, axis=1).reshape(
        flat_rows.shape[0], blocks_here, slots, row_width
    )
    partial_terms = jnp.einsum(
        "qlr,qlsc->lsrc", own_blocks, partner_rows, preferred_element_type=jnp.float32
    )
    my_sums = lax.psum_scatter(partial_terms, "pair", scatter_dimension=2, tiled=True)
    row_count = my_sums.shape[2]
    row_start = lax.axis_index("pair") * row_count
    block_ids = first_block + jnp.arange(blocks_here, dtype=jnp.int32)
    row_vals = (
        jnp.take(occ_energy, block_ids, axis=0)[:, :, None]
        - jnp.take(vir_energy, jnp.take(domains, block_ids, axis=0), axis=0)[:, None, :]
    )
    row_vals = lax.dynamic_slice_in_dim(
        row_vals.reshape(blocks_here, row_width), row_start, row_count, 1
    )
    col_vals = (
        jnp.take(occ_energy, partners, axis=0)[:, :, :, None]
        - jnp.take(vir_energy, jnp.take(domains, partners, axis=0), axis=0)[:, :, None, :]
    )
    col_vals = col_vals.reshape(blocks_here, slots, row_width)
    denominator = row_vals[:, None, :, None] + col_vals[:, :, None, :]
    amplitudes = my_sums / denominator
    weighted = (
        (my_sums * amplitudes).reshape(blocks_here, slots, row_count, orbitals, domain).sum(axis=4)
    )
    orbital_of = (row_start + jnp.arange(row_count, dtype=jnp.int32)) // domain
    selector = (orbital_of[:, None] == jnp.arange(orbitals, dtype=jnp.int32)[None, :]).astype(
        jnp.float32
    )
    partial_energy = jnp.einsum(
        "lskj,ki->lsij", weighted, selector, precision=lax.Precision.HIGHEST
    )
    pair_energy = lax.psum(partial_energy, "pair") / (domain * domain)
    return (amplitudes, pair_energy)


def on_device(half_ints, partners, domains, occ_energy, vir_energy):
    _, _, orbitals, domain = half_ints.shape
    fits = partners.shape[0] == 2 and domain == 128 and vir_energy.shape[0] % domain == 0
    fits &= lax.axis_size("pair") == lax.axis_size("aux") == orbitals == 4
    step = fast if fits and half_ints.shape[0] % 16 == 0 else general
    return step(half_ints, partners, domains, occ_energy, vir_energy)


def solution(mesh):
    return jax.shard_map(
        on_device,
        mesh=mesh,
        in_specs=(
            P(("frag", "aux", "pair"), None, None, None),
            P(("frag", "aux"), None),
            P("frag", None),
            P("frag", None),
            P("frag"),
        ),
        out_specs=(P(("frag", "aux"), None, "pair", None), P(("frag", "aux"), None, None, None)),
        check_vma=False,
    )
```

```python
import jax
import jax.numpy as jnp
from jax import lax
from jax.experimental import pallas as pl
from jax.experimental.pallas import tpu as pltpu
from jax.sharding import PartitionSpec as P

BF16, F16, F32 = jnp.bfloat16, jnp.float16, jnp.float32
VMEM = pl.BlockSpec(memory_space=pltpu.VMEM)
SMEM = pl.BlockSpec(memory_space=pltpu.SMEM)
ANY = pl.BlockSpec(memory_space=pl.ANY)
PARAMS = pltpu.CompilerParams(vmem_limit_bytes=8 * 2**20)
PEAK_ROWS = 16
GROUPS = ([[(0, 1)]], [[(1, 1), (0, 2), (1, 2)]])

def shape(*dims, dtype=F32):
    return jax.ShapeDtypeStruct(dims, dtype)


def call(kernel, name, **options):
    return pl.pallas_call(kernel, compiler_params=PARAMS, name=name, **options)


def after(value, *others):
    return lax.optimization_barrier((value, *others))[0]


def panel_at(depth, orbital, block):
    return pl.ds((orbital * 2 + block) * depth, depth)


def depth_of(one_set, orbitals):
    return (one_set.shape[0] - PEAK_ROWS) // (2 * orbitals)


def pack(raw, count):
    depth, blocks, orbitals, domain = raw.shape
    rows, parts = blocks * orbitals, 4
    part = depth * rows // parts

    def kernel(raw_ref, *refs):
        outs, wide = refs[:count], refs[-1]
        z = lax.axis_index("aux")
        wide[...] = raw_ref[...].astype(F32)
        peak = jnp.max(jnp.abs(wide[...]).reshape(-1, PEAK_ROWS, domain), axis=0)
        for k in range(count):
            out = outs[(k + 1) % count]
            block = 2 * jnp.bitwise_xor(z, (k + 1) % count)
            for r in range(2):
                for i in range(orbitals):
                    at = pl.ds((block + r) * orbitals + i, depth, stride=rows)
                    out[panel_at(depth, i, r), :] = wide[at, :].astype(BF16)
            out[2 * orbitals * depth :, :] = peak.astype(BF16)

    one_set = shape(2 * orbitals * depth + PEAK_ROWS, domain, dtype=BF16)
    return call(
        kernel,
        "pack",
        out_shape=[one_set] * count,
        in_specs=[VMEM],
        out_specs=[VMEM] * count,
        scratch_shapes=[
            pltpu.VMEM((depth * rows, domain), F32),
        ],
    )(raw.reshape(depth * rows, domain))


def relay(own, rows):
    domain = own[0].shape[1]

    def kernel(*refs):
        own_refs, outs = refs[:4], refs[4:]
        for out, partner in zip(outs, (1, 3)):
            for k in (1, 2, 3):
                out[(k - 1) * rows : k * rows] = own_refs[k ^ partner][:rows]

    return call(
        kernel,
        "relay",
        out_shape=[shape(3 * rows, domain, dtype=BF16)] * 2,
        in_specs=[VMEM] * 4,
        out_specs=[VMEM] * 2,
    )(*own)


def product(left, right):
    return lax.dot_general(left, right, (((0,), (0,)), ((), ())), preferred_element_type=F32)


def left_rows(own_refs, depth, r):
    p = lax.axis_index("pair")
    x, c = p // 2, lax.rem(p, 2)
    order = (2 * x + c, 2 * (1 - x) + c, 2 * x + 1 - c, 2 * (1 - x) + 1 - c)
    columns = [
        jnp.concatenate([ref[panel_at(depth, i, r), :] for ref in own_refs], axis=0) for i in order
    ]
    return jnp.concatenate(columns, axis=1)


def store_sums(sums, at, mine, other, give):
    domain = sums.shape[0] // 4
    mine[at] = sums[:domain]
    other[at] = sums[domain : 2 * domain]
    give[0, at] = sums[2 * domain : 3 * domain]
    give[1, at] = sums[3 * domain :]


def own_pairs(own, orbitals):
    count, domain = len(own), own[0].shape[1]
    depth = depth_of(own[0], orbitals)
    wide = orbitals * domain

    def kernel(*refs):
        own_refs, (mine, other, give, peak) = refs[:count], refs[count:]
        top = own_refs[0][-PEAK_ROWS:, :].astype(F32)
        for ref in own_refs[1:]:
            top = jnp.maximum(top, ref[-PEAK_ROWS:, :].astype(F32))
        top = jnp.maximum(top[:8], top[8:])
        peak[...] = jnp.concatenate([top] * orbitals, axis=1)
        for n in range(2):
            give[n, 2 * domain :] = peak[...]
        for r in range(2):
            right = jnp.concatenate(
                [
                    jnp.concatenate([ref[panel_at(depth, j, r), :] for ref in own_refs], axis=0)
                    for j in range(orbitals)
                ],
                axis=1,
            )
            at = slice(r * domain, (r + 1) * domain)
            store_sums(product(left_rows(own_refs, depth, r), right), at, mine, other, give)

    return call(
        kernel,
        "own",
        out_shape=[
            shape(2 * domain, wide),
            shape(2 * domain, wide),
            shape(2, 2 * domain + 8, wide),
            shape(8, wide),
        ],
        in_specs=[VMEM] * count,
        out_specs=[VMEM] * 4,
    )(*own)


def near_pairs(partners, own, here, sides, orbitals, groups):
    count, domain = len(own), own[0].shape[1]
    depth = depth_of(own[0], orbitals)
    rows, wide = 2 * orbitals * depth, orbitals * domain

    def kernel(partners_ref, *refs):
        own_refs, here_refs, side_refs = refs[:count], refs[count : count + 2], refs[count + 2 :][:2]
        z = lax.axis_index("aux")

        def panels(r, j, slot):
            if slot == 1:
                w = (partners_ref[r : r + 1, slot : slot + 1] if only_first else partners_ref[r, slot]) - 2 * z + 2
                from_first = jnp.where(w > 3, 1, 0) != lax.rem(z, 2)
                from_first = jnp.broadcast_to(from_first, (depth, domain))
                at = (2 * j + r) * depth
            else:
                w = partners_ref[r, slot] - 2 * z + 2
                from_first = (w > 3) == (lax.rem(z, 2) == 0)
                at = (2 * j + lax.rem(w, 2)) * depth
            found = []
            for k in range(count):
                refs, start = (here_refs, at) if k == 0 else (side_refs, at + (k - 1) * rows)
                rows_at = pl.ds(pl.multiple_of(start, 16), depth)
                panel = jnp.where(from_first, refs[0][rows_at, :], refs[1][rows_at, :])
                if slot > 1:
                    own_at = pl.ds(pl.multiple_of(at, 16), depth)
                    panel = jnp.where((w == 2) | (w == 3), own_refs[k][own_at, :], panel)
                found.append(panel)
            return jnp.concatenate(found, axis=0)

        for n, tiles in enumerate(groups):
            for t, (r, slot) in enumerate(tiles):
                right = jnp.concatenate([panels(r, j, slot) for j in range(orbitals)], axis=1)
                sums = product(left_rows(own_refs, depth, r), right)
                at = slice(t * domain, (t + 1) * domain)
                store_sums(sums, at, *refs[count + 4 + 3 * n :][:3])

    only_first = all(slot == 1 for tiles in groups for _, slot in tiles)
    outs = []
    for tiles in groups:
        height = len(tiles) * domain
        outs += [shape(height, wide), shape(height, wide), shape(2, height, wide)]
    return call(
        kernel,
        "near",
        out_shape=outs,
        in_specs=[VMEM if only_first else SMEM] + [VMEM] * (count + 4),
        out_specs=[VMEM] * len(outs),
    )(partners, *own, *here, *sides)


def scale_down(peak, got, depth):
    def kernel(peak_ref, got_ref, top_ref, down_ref):
        top = jnp.maximum(peak_ref[...], got_ref[0, -8:])
        top_ref[...] = top
        top = jnp.maximum(jnp.max(top[:, :128], axis=(0, 1), keepdims=True), 1e-17)
        down_ref[...] = jnp.broadcast_to(32768.0 / (top * top * depth), down_ref.shape)

    return call(
        kernel,
        "scale_down",
        out_shape=[shape(*peak.shape)] * 2,
        in_specs=[VMEM] * 2,
        out_specs=[VMEM] * 2,
    )(peak, got)


def scale_up(top, depth):
    def kernel(top_ref, up_ref):
        top = jnp.maximum(jnp.max(top_ref[:, :128], axis=(0, 1), keepdims=True), 1e-17)
        up_ref[...] = jnp.broadcast_to((top * top * depth) * (1.0 / 32768.0), up_ref.shape)

    return call(
        kernel, "scale_up", out_shape=shape(*top.shape), in_specs=[VMEM], out_specs=VMEM
    )(top)


def amplitude_tiles(total_ref, row_ref, col_ref, amp, energy_ref, tiles, done):
    rows, wide = amp.shape[1:]
    for t, (r, slot) in enumerate(tiles):
        row = row_ref[r]
        for j in range(wide // rows):
            at = slice(j * rows, (j + 1) * rows)
            total = total_ref[t * rows : (t + 1) * rows, at]
            tile = total / (row + col_ref[r, slot, j : j + 1, :])
            amp[t, :, at] = tile
            energy_ref[t, j : j + 1, :] = jnp.sum(total * tile, axis=0, keepdims=True)
        done(t)


def finish(totals, row_vals, col_vals, tiles, before, out):
    rows, wide = out[2:]
    count = len(tiles)

    def kernel(total_ref, row_ref, col_ref, *refs):
        amp_ref, energy_ref, amp, sems = refs[-4:]
        copies = []

        def done(t):
            r, slot = tiles[t]
            copies.append(pltpu.make_async_copy(amp.at[t], amp_ref.at[r, slot], sems.at[t]))
            copies[-1].start()

        amplitude_tiles(total_ref, row_ref, col_ref, amp, energy_ref, tiles, done)
        for started in copies:
            started.wait()

    return call(
        kernel,
        "finish",
        out_shape=[shape(*out), shape(count, wide // rows, rows)],
        in_specs=[VMEM] * 3 + [ANY] * len(before),
        out_specs=[ANY, VMEM],
        input_output_aliases={3: 0} if before else {},
        scratch_shapes=[pltpu.VMEM((count, rows, wide), F32), pltpu.SemaphoreType.DMA((count,))],
    )(totals, row_vals, col_vals, *before)


def finish_last(totals, row_vals, col_vals, tiles, before, shares):
    orbitals, domain = col_vals.shape[2:]
    wide = orbitals * domain
    blocks, slots = col_vals.shape[:2]
    count = len(tiles)
    known = len(shares)

    def kernel(total_ref, row_ref, col_ref, *refs):
        share_refs, (amp_ref, out, energy) = refs[:known], refs[known:]
        amplitude_tiles(total_ref, row_ref, col_ref, amp_ref, energy, tiles, lambda t: None)
        p = lax.axis_index("pair")
        row = lax.broadcasted_iota(jnp.int32, (orbitals, orbitals), 0)
        column = lax.broadcasted_iota(jnp.int32, (orbitals, orbitals), 1)
        for ref, places in zip((*share_refs, energy), (*before, tiles)):
            for t, (r, slot) in enumerate(places):
                sums = jnp.sum(ref[t], axis=1, keepdims=True) * (1.0 / (domain * domain))
                value = jnp.zeros((orbitals, orbitals), F32)
                for j in range(orbitals):
                    value = jnp.where((row == p) & (column == j), sums[j : j + 1, :], value)
                out[r, slot] = value

    return call(
        kernel,
        "finish_last",
        out_shape=[shape(count, domain, wide), shape(blocks, slots, orbitals, orbitals)],
        in_specs=[VMEM] * (3 + known),
        out_specs=[VMEM] * 2,
        scratch_shapes=[pltpu.VMEM((count, orbitals, domain), F32)],
    )(totals, row_vals, col_vals, *shares)


def put(tiles_at, values, amps):
    def kernel(values_ref, _, amp_ref, sems):
        copies = []
        for t, (r, slot) in enumerate(tiles_at):
            copies.append(pltpu.make_async_copy(values_ref.at[t], amp_ref.at[r, slot], sems.at[t]))
            copies[-1].start()
        for started in copies:
            started.wait()

    return call(
        kernel,
        "put",
        out_shape=shape(*amps.shape),
        in_specs=[VMEM, ANY],
        out_specs=ANY,
        input_output_aliases={1: 0},
        scratch_shapes=[pltpu.SemaphoreType.DMA((len(tiles_at),))],
    )(values, amps)


def last(shares):
    def kernel(*refs):
        refs[4][...] = (refs[0][...] + refs[1][...]) + (refs[2][...] + refs[3][...])

    return call(
        kernel,
        "last",
        out_shape=shape(*shares[0].shape),
        in_specs=[VMEM] * 4,
        out_specs=VMEM,
    )(*shares)


def energies(partners, domains, occ_energy, vir_energy):
    blocks, domain = domains.shape
    orbitals = occ_energy.shape[1]
    here, slots = partners.shape
    tables = vir_energy.shape[0] // domain

    def kernel(partners_ref, occ_ref, domains_ref, vir_ref, row_ref, col_ref, picked):
        at = domains_ref[...]
        lane, table = lax.rem(at, domain), lax.div(at, domain)
        vir = jnp.zeros(at.shape, F32)
        for t in range(tables):
            values = jnp.broadcast_to(vir_ref[t : t + 1, :], at.shape)
            vir = jnp.where(table == t, jnp.take_along_axis(values, lane, axis=1), vir)
        picked[...] = vir
        z, p = lax.axis_index("aux"), lax.axis_index("pair")
        for r in range(here):
            block = here * z + r
            value = occ_ref[p, block] - picked[pl.ds(block, 1), :]
            row_ref[r] = jnp.broadcast_to(value, (domain, domain)).T
            for s in range(slots):
                other = partners_ref[r, s]
                value = picked[pl.ds(other, 1), :]
                for j in range(orbitals):
                    col_ref[r, s, j : j + 1, :] = occ_ref[j, other] - value

    return call(
        kernel,
        "energies",
        out_shape=[shape(here, domain, domain), shape(here, slots, orbitals, domain)],
        in_specs=[SMEM] * 2 + [VMEM] * 2,
        out_specs=[VMEM] * 2,
        scratch_shapes=[pltpu.VMEM((blocks, domain), F32)],
    )(partners, occ_energy.T, domains, vir_energy.reshape(tables, domain))


def fast(half_ints, partners, domains, occ_energy, vir_energy):
    depth, _, orbitals, domain = half_ints.shape
    count = lax.axis_size("aux")
    wide = orbitals * domain
    sides = [[(i, i ^ 4) for i in range(16)], [(i, i ^ (12 if 4 <= i < 12 else 1)) for i in range(16)]]
    swap, cross, both = ([(i, i ^ k) for i in range(4)] for k in (1, 2, 3))

    own_here, *sends = pack(half_ints, count)
    here = [sends[0], sends[2]]
    own = [own_here]
    for k, send in enumerate(sends, 1):
        own.append(lax.ppermute(send, "aux", [(i, i ^ k) for i in range(count)]))
    row_vals, col_vals = energies(partners, domains, occ_energy, vir_energy)
    messages = relay(own, 2 * orbitals * depth)
    near = [lax.ppermute(m, ("aux", "pair"), side) for m, side in zip(messages, sides)]
    own[0] = after(own[0], *messages)

    def across_cores(mine, other, give):
        got = lax.ppermute(give, "pair", swap)
        height = mine.shape[0]
        return mine, got, other + got[1, :height]

    def across_chips(other):
        return lax.ppermute((other * to_half[:1]).astype(F16), "pair", cross)

    *sums, peak = own_pairs(own, orbitals)
    mine, got, other = across_cores(*sums)
    top, to_half = scale_down(peak, got, 2 * count * depth)
    parts = [(mine, got, across_chips(other))]
    from_half = scale_up(lax.ppermute(top, "pair", cross), 2 * count * depth)
    here[0] = after(here[0], parts[0][2], from_half, row_vals)

    groups = [[(0, 0), (1, 0)], *GROUPS[0], *GROUPS[1]]
    sums = near_pairs(partners, own, here, near, orbitals, GROUPS[0])
    here[0] = after(here[0], sums[0])
    sums += near_pairs(partners, own, here, near, orbitals, GROUPS[1])
    for n in range(0, len(sums), 3):
        mine, other, give = sums[n : n + 3]
        if n:
            give = after(give, half)
        mine, got, other = across_cores(mine, other, give)
        half = (other * to_half[:1]).astype(F16)
        parts.append((mine, got, lax.ppermute(half, "pair", cross)))

    out = partners.shape + (domain, wide)
    amps, shares = [], []
    for at, (mine, got, across) in enumerate(parts):
        back = after(from_half, shares[-1]) if at else from_half
        total = mine + got[0, : mine.shape[0]] + across.astype(F32) * back[:1]
        if at < len(parts) - 1:
            *amps, share = finish(total, row_vals, col_vals, groups[at], amps, out)
            shares.append(share)
    values, share = finish_last(total, row_vals, col_vals, groups[-1], groups[:-1], shares)
    others = [lax.ppermute(share, "pair", to) for to in (swap, cross, both)]
    return put(groups[-1], values, amps[0]), last([share, *others])


def padded(shard, sides, width):
    for axis, dim in sides:
        size, length = (lax.axis_size(axis), shard.shape[dim])
        up = [(i, (i + 1) % size) for i in range(size - 1)]
        down = [(j, i) for i, j in up]
        last = lax.slice_in_dim(shard, length - width, length, axis=dim)
        first = lax.slice_in_dim(shard, 0, width, axis=dim)
        before = lax.ppermute(last, axis, up)
        after = lax.ppermute(first, axis, down)
        shard = jnp.concatenate([before, shard, after], axis=dim)
    return shard


def general(half_ints, partners, domains, occ_energy, vir_energy):
    blocks_here, slots = partners.shape
    orbitals = half_ints.shape[2]
    domain = half_ints.shape[3]
    row_width = orbitals * domain
    first_block = lax.axis_index("aux") * blocks_here
    owned = lax.all_to_all(half_ints, "aux", split_axis=1, concat_axis=0, tiled=True)
    widened = padded(owned, (("aux", 1),), blocks_here)
    flat_rows = widened.reshape(widened.shape[0], 3 * blocks_here, row_width)
    own_blocks = flat_rows[:, blocks_here : 2 * blocks_here]
    positions = (partners - first_block + blocks_here).reshape(-1)
    partner_rows = jnp.take(flat_rows, positions, axis=1).reshape(
        flat_rows.shape[0], blocks_here, slots, row_width
    )
    partial_terms = jnp.einsum(
        "qlr,qlsc->lsrc", own_blocks, partner_rows, preferred_element_type=jnp.float32
    )
    my_sums = lax.psum_scatter(partial_terms, "pair", scatter_dimension=2, tiled=True)
    row_count = my_sums.shape[2]
    row_start = lax.axis_index("pair") * row_count
    block_ids = first_block + jnp.arange(blocks_here, dtype=jnp.int32)
    row_vals = (
        jnp.take(occ_energy, block_ids, axis=0)[:, :, None]
        - jnp.take(vir_energy, jnp.take(domains, block_ids, axis=0), axis=0)[:, None, :]
    )
    row_vals = lax.dynamic_slice_in_dim(
        row_vals.reshape(blocks_here, row_width), row_start, row_count, 1
    )
    col_vals = (
        jnp.take(occ_energy, partners, axis=0)[:, :, :, None]
        - jnp.take(vir_energy, jnp.take(domains, partners, axis=0), axis=0)[:, :, None, :]
    )
    col_vals = col_vals.reshape(blocks_here, slots, row_width)
    denominator = row_vals[:, None, :, None] + col_vals[:, :, None, :]
    amplitudes = my_sums / denominator
    weighted = (
        (my_sums * amplitudes).reshape(blocks_here, slots, row_count, orbitals, domain).sum(axis=4)
    )
    orbital_of = (row_start + jnp.arange(row_count, dtype=jnp.int32)) // domain
    selector = (orbital_of[:, None] == jnp.arange(orbitals, dtype=jnp.int32)[None, :]).astype(
        jnp.float32
    )
    partial_energy = jnp.einsum(
        "lskj,ki->lsij", weighted, selector, precision=lax.Precision.HIGHEST
    )
    pair_energy = lax.psum(partial_energy, "pair") / (domain * domain)
    return (amplitudes, pair_energy)


def on_device(half_ints, partners, domains, occ_energy, vir_energy):
    _, _, orbitals, domain = half_ints.shape
    fits = partners.shape[0] == 2 and domain == 128 and vir_energy.shape[0] % domain == 0
    fits &= lax.axis_size("pair") == lax.axis_size("aux") == orbitals == 4
    step = fast if fits and half_ints.shape[0] % 16 == 0 else general
    return step(half_ints, partners, domains, occ_energy, vir_energy)


def solution(mesh):
    return jax.shard_map(
        on_device,
        mesh=mesh,
        in_specs=(
            P(("frag", "aux", "pair"), None, None, None),
            P(("frag", "aux"), None),
            P("frag", None),
            P("frag", None),
            P("frag"),
        ),
        out_specs=(P(("frag", "aux"), None, "pair", None), P(("frag", "aux"), None, None, None)),
        check_vma=False,
    )
```

```python
import jax
import jax.numpy as jnp
from jax import lax
from jax.experimental import pallas as pl
from jax.experimental.pallas import tpu as pltpu
from jax.sharding import PartitionSpec as P

BF16, F16, F32 = jnp.bfloat16, jnp.float16, jnp.float32
VMEM = pl.BlockSpec(memory_space=pltpu.VMEM)
SMEM = pl.BlockSpec(memory_space=pltpu.SMEM)
ANY = pl.BlockSpec(memory_space=pl.ANY)
PARAMS = pltpu.CompilerParams(vmem_limit_bytes=8 * 2**20)
PEAK_ROWS = 16
GROUPS = ([[(0, 1)]], [[(1, 1), (0, 2), (1, 2)]])

def shape(*dims, dtype=F32):
    return jax.ShapeDtypeStruct(dims, dtype)


def call(kernel, name, **options):
    return pl.pallas_call(kernel, compiler_params=PARAMS, name=name, **options)


def after(value, *others):
    return lax.optimization_barrier((value, *others))[0]


def panel_at(depth, orbital, block):
    return pl.ds((orbital * 2 + block) * depth, depth)


def depth_of(one_set, orbitals):
    return (one_set.shape[0] - PEAK_ROWS) // (2 * orbitals)


def pack(raw, count):
    depth, blocks, orbitals, domain = raw.shape
    rows = blocks * orbitals
    group = rows // 2

    def kernel(raw_ref, *refs):
        outs, (narrow, wide, sems) = refs[:count], refs[count:]
        z = lax.axis_index("aux")
        copies = []
        for n in range(2):
            start = pl.multiple_of((lax.div(z, 2) ^ (1 - n)) * group, 16)
            part = raw_ref.at[:, pl.ds(start, group), :]
            copies.append(pltpu.make_async_copy(part, narrow.at[n], sems.at[n]))
            copies[-1].start()
        peak = jnp.zeros((PEAK_ROWS, domain), F32)
        for n, ks in enumerate(((2, 3), (0, 1))):
            copies[n].wait()
            values = narrow[n].astype(F32).reshape(depth * group, domain)
            wide[n] = values
            values = jnp.max(jnp.abs(values).reshape(-1, PEAK_ROWS, domain), axis=0)
            peak = jnp.maximum(peak, values)
            for k in ks:
                first = lax.rem(z ^ k, 2) * 2 * orbitals
                for r in range(2):
                    for i in range(orbitals):
                        at = pl.ds(first + r * orbitals + i, depth, stride=group)
                        outs[k][panel_at(depth, i, r), :] = wide[n, at, :].astype(BF16)
        for out in outs:
            out[2 * orbitals * depth :, :] = peak.astype(BF16)

    one_set = shape(2 * orbitals * depth + PEAK_ROWS, domain, dtype=BF16)
    return call(
        kernel,
        "pack",
        out_shape=[one_set] * count,
        in_specs=[pl.BlockSpec(memory_space=pltpu.HBM)],
        out_specs=[VMEM] * count,
        scratch_shapes=[
            pltpu.VMEM((2, depth, group, domain), BF16),
            pltpu.VMEM((2, depth * group, domain), F32),
            pltpu.SemaphoreType.DMA((2,)),
        ],
    )(pltpu.with_memory_space_constraint(raw.reshape(depth, rows, domain), pltpu.HBM))


def relay(own, rows):
    domain = own[0].shape[1]

    def kernel(*refs):
        own_refs, outs = refs[:4], refs[4:]
        for out, partner in zip(outs, (1, 3)):
            for k in (1, 2, 3):
                out[(k - 1) * rows : k * rows] = own_refs[k ^ partner][:rows]

    return call(
        kernel,
        "relay",
        out_shape=[shape(3 * rows, domain, dtype=BF16)] * 2,
        in_specs=[VMEM] * 4,
        out_specs=[VMEM] * 2,
    )(*own)


def product(left, right):
    return lax.dot_general(left, right, (((0,), (0,)), ((), ())), preferred_element_type=F32)


def left_rows(own_refs, depth, r):
    p = lax.axis_index("pair")
    x, c = p // 2, lax.rem(p, 2)
    order = (2 * x + c, 2 * (1 - x) + c, 2 * x + 1 - c, 2 * (1 - x) + 1 - c)
    columns = [
        jnp.concatenate([ref[panel_at(depth, i, r), :] for ref in own_refs], axis=0) for i in order
    ]
    return jnp.concatenate(columns, axis=1)


def store_sums(sums, at, *outs):
    domain = sums.shape[0] // 4
    for n, out in enumerate(outs):
        out[at] = sums[n * domain : (n + 1) * domain]


def own_pairs(own, orbitals):
    count, domain = len(own), own[0].shape[1]
    depth = depth_of(own[0], orbitals)
    wide = orbitals * domain

    def kernel(*refs):
        own_refs, (mine, other, give, peak) = refs[:count], refs[count:]
        top = own_refs[0][-PEAK_ROWS:, :].astype(F32)
        for ref in own_refs[1:]:
            top = jnp.maximum(top, ref[-PEAK_ROWS:, :].astype(F32))
        top = jnp.maximum(top[:8], top[8:])
        peak[...] = jnp.concatenate([top] * orbitals, axis=1)
        for n in range(2):
            give[n, 2 * domain :] = peak[...]
        for r in range(2):
            right = jnp.concatenate(
                [
                    jnp.concatenate([ref[panel_at(depth, j, r), :] for ref in own_refs], axis=0)
                    for j in range(orbitals)
                ],
                axis=1,
            )
            at = slice(r * domain, (r + 1) * domain)
            store_sums(product(left_rows(own_refs, depth, r), right), at, mine, other, give.at[0], give.at[1])

    return call(
        kernel,
        "own",
        out_shape=[
            shape(2 * domain, wide),
            shape(2 * domain, wide),
            shape(2, 2 * domain + 8, wide),
            shape(8, wide),
        ],
        in_specs=[VMEM] * count,
        out_specs=[VMEM] * 4,
    )(*own)


def near_pairs(partners, own, here, sides, orbitals, groups):
    count, domain = len(own), own[0].shape[1]
    depth = depth_of(own[0], orbitals)
    rows, wide = 2 * orbitals * depth, orbitals * domain

    def kernel(partners_ref, *refs):
        own_refs, here_refs, side_refs = refs[:count], refs[count : count + 2], refs[count + 2 :][:2]
        outs = refs[count + 4 :]
        z = lax.axis_index("aux")

        def flag(value):
            return jnp.broadcast_to(value, (depth, domain))

        def panels(r, j, slot, w):
            from_first = flag(jnp.where(w > 3, 1, 0) != lax.rem(z, 2))
            is_own, is_second = flag((w == 2) | (w == 3)), flag(lax.rem(w, 2) == 1)

            def either(first, second, start):
                rows_at = slice(start, start + depth)
                return jnp.where(from_first, first[rows_at, :], second[rows_at, :])

            found = []
            for k in range(count):
                refs, start = (here_refs, 0) if k == 0 else (side_refs, (k - 1) * rows)
                start += 2 * j * depth
                if slot == 1:
                    panel = either(*refs, start + r * depth)
                else:
                    panel = jnp.where(is_second, either(*refs, start + depth), either(*refs, start))
                    mine = [own_refs[k][panel_at(depth, j, block), :] for block in range(2)]
                    panel = jnp.where(is_own, jnp.where(is_second, mine[1], mine[0]), panel)
                found.append(panel)
            return jnp.concatenate(found, axis=0)

        for n, tiles in enumerate(groups):
            for t, (r, slot) in enumerate(tiles):
                w = partners_ref[r : r + 1, slot : slot + 1] - 2 * z + 2
                right = jnp.concatenate([panels(r, j, slot, w) for j in range(orbitals)], axis=1)
                sums = product(left_rows(own_refs, depth, r), right)
                at = slice(t * domain, (t + 1) * domain)
                store_sums(sums, at, *outs[4 * n : 4 * n + 4])

    shapes = []
    for tiles in groups:
        shapes += [shape(len(tiles) * domain, wide)] * 4
    return call(
        kernel,
        "near",
        out_shape=shapes,
        in_specs=[VMEM] * (count + 5),
        out_specs=[VMEM] * len(shapes),
    )(partners, *own, *here, *sides)


def scale_down(peak, got, depth):
    def kernel(peak_ref, got_ref, top_ref, down_ref):
        top = jnp.maximum(peak_ref[...], got_ref[0, -8:])
        top_ref[...] = top
        top = jnp.maximum(jnp.max(top[:, :128], axis=(0, 1), keepdims=True), 1e-17)
        down_ref[...] = jnp.broadcast_to(32768.0 / (top * top * depth), down_ref.shape)

    return call(
        kernel,
        "scale_down",
        out_shape=[shape(*peak.shape)] * 2,
        in_specs=[VMEM] * 2,
        out_specs=[VMEM] * 2,
    )(peak, got)


def scale_up(top, depth):
    def kernel(top_ref, up_ref):
        top = jnp.maximum(jnp.max(top_ref[:, :128], axis=(0, 1), keepdims=True), 1e-17)
        up_ref[...] = jnp.broadcast_to((top * top * depth) * (1.0 / 32768.0), up_ref.shape)

    return call(
        kernel, "scale_up", out_shape=shape(*top.shape), in_specs=[VMEM], out_specs=VMEM
    )(top)


def amplitude_tiles(total_ref, row_ref, col_ref, amp, energy_ref, tiles, done):
    rows, wide = amp.shape[1:]
    for t, (r, slot) in enumerate(tiles):
        row = row_ref[r]
        for j in range(wide // rows):
            at = slice(j * rows, (j + 1) * rows)
            total = total_ref[t * rows : (t + 1) * rows, at]
            tile = total / (row + col_ref[r, slot, j : j + 1, :])
            amp[t, :, at] = tile
            energy_ref[t, j : j + 1, :] = jnp.sum(total * tile, axis=0, keepdims=True)
        done(t)


def finish(totals, row_vals, col_vals, tiles, before, out):
    rows, wide = out[2:]
    count = len(tiles)

    def kernel(total_ref, row_ref, col_ref, *refs):
        amp_ref, energy_ref, amp, sems = refs[-4:]
        copies = []

        def done(t):
            r, slot = tiles[t]
            copies.append(pltpu.make_async_copy(amp.at[t], amp_ref.at[r, slot], sems.at[t]))
            copies[-1].start()

        amplitude_tiles(total_ref, row_ref, col_ref, amp, energy_ref, tiles, done)
        for started in copies:
            started.wait()

    return call(
        kernel,
        "finish",
        out_shape=[shape(*out), shape(count, wide // rows, rows)],
        in_specs=[VMEM] * 3 + [ANY] * len(before),
        out_specs=[ANY, VMEM],
        input_output_aliases={3: 0} if before else {},
        scratch_shapes=[pltpu.VMEM((count, rows, wide), F32), pltpu.SemaphoreType.DMA((count,))],
    )(totals, row_vals, col_vals, *before)


def finish_last(totals, row_vals, col_vals, tiles, before, shares):
    orbitals, domain = col_vals.shape[2:]
    wide = orbitals * domain
    blocks, slots = col_vals.shape[:2]
    count = len(tiles)
    known = len(shares)

    def kernel(total_ref, row_ref, col_ref, *refs):
        share_refs, (amp_ref, out, energy) = refs[:known], refs[known:]
        amplitude_tiles(total_ref, row_ref, col_ref, amp_ref, energy, tiles, lambda t: None)
        p = lax.axis_index("pair")
        row = lax.broadcasted_iota(jnp.int32, (orbitals, orbitals), 0)
        column = lax.broadcasted_iota(jnp.int32, (orbitals, orbitals), 1)
        for ref, places in zip((*share_refs, energy), (*before, tiles)):
            for t, (r, slot) in enumerate(places):
                sums = jnp.sum(ref[t], axis=1, keepdims=True) * (1.0 / (domain * domain))
                value = jnp.zeros((orbitals, orbitals), F32)
                for j in range(orbitals):
                    value = jnp.where((row == p) & (column == j), sums[j : j + 1, :], value)
                out[r, slot] = value

    return call(
        kernel,
        "finish_last",
        out_shape=[shape(count, domain, wide), shape(blocks, slots, orbitals, orbitals)],
        in_specs=[VMEM] * (3 + known),
        out_specs=[VMEM] * 2,
        scratch_shapes=[pltpu.VMEM((count, orbitals, domain), F32)],
    )(totals, row_vals, col_vals, *shares)


def put(tiles_at, values, amps):
    def kernel(values_ref, _, amp_ref, sems):
        copies = []
        for t, (r, slot) in enumerate(tiles_at):
            copies.append(pltpu.make_async_copy(values_ref.at[t], amp_ref.at[r, slot], sems.at[t]))
            copies[-1].start()
        for started in copies:
            started.wait()

    return call(
        kernel,
        "put",
        out_shape=shape(*amps.shape),
        in_specs=[VMEM, ANY],
        out_specs=ANY,
        input_output_aliases={1: 0},
        scratch_shapes=[pltpu.SemaphoreType.DMA((len(tiles_at),))],
    )(values, amps)


def last(shares):
    def kernel(*refs):
        refs[4][...] = (refs[0][...] + refs[1][...]) + (refs[2][...] + refs[3][...])

    return call(
        kernel,
        "last",
        out_shape=shape(*shares[0].shape),
        in_specs=[VMEM] * 4,
        out_specs=VMEM,
    )(*shares)


def energies(partners, domains, occ_energy, vir_energy):
    blocks, domain = domains.shape
    orbitals = occ_energy.shape[1]
    here, slots = partners.shape
    tables = vir_energy.shape[0] // domain

    def kernel(partners_ref, occ_ref, domains_ref, vir_ref, row_ref, col_ref, picked):
        at = domains_ref[...]
        lane, table = lax.rem(at, domain), lax.div(at, domain)
        vir = jnp.zeros(at.shape, F32)
        for t in range(tables):
            values = jnp.broadcast_to(vir_ref[t : t + 1, :], at.shape)
            vir = jnp.where(table == t, jnp.take_along_axis(values, lane, axis=1), vir)
        picked[...] = vir
        z, p = lax.axis_index("aux"), lax.axis_index("pair")
        for r in range(here):
            block = here * z + r
            value = occ_ref[p, block] - picked[pl.ds(block, 1), :]
            row_ref[r] = jnp.broadcast_to(value, (domain, domain)).T
            for s in range(slots):
                other = partners_ref[r, s]
                value = picked[pl.ds(other, 1), :]
                for j in range(orbitals):
                    col_ref[r, s, j : j + 1, :] = occ_ref[j, other] - value

    return call(
        kernel,
        "energies",
        out_shape=[shape(here, domain, domain), shape(here, slots, orbitals, domain)],
        in_specs=[SMEM] * 2 + [VMEM] * 2,
        out_specs=[VMEM] * 2,
        scratch_shapes=[pltpu.VMEM((blocks, domain), F32)],
    )(partners, occ_energy.T, domains, vir_energy.reshape(tables, domain))


def fast(half_ints, partners, domains, occ_energy, vir_energy):
    depth, _, orbitals, domain = half_ints.shape
    count = lax.axis_size("aux")
    wide = orbitals * domain
    sides = [[(i, i ^ 4) for i in range(16)], [(i, i ^ (12 if 4 <= i < 12 else 1)) for i in range(16)]]
    swap, cross, both = ([(i, i ^ k) for i in range(4)] for k in (1, 2, 3))

    own_here, *sends = pack(half_ints, count)
    here = [sends[0], sends[2]]
    own = [own_here]
    for k, send in enumerate(sends, 1):
        own.append(lax.ppermute(send, "aux", [(i, i ^ k) for i in range(count)]))
    row_vals, col_vals = energies(partners, domains, occ_energy, vir_energy)
    messages = relay(own, 2 * orbitals * depth)
    near = [lax.ppermute(m, ("aux", "pair"), side) for m, side in zip(messages, sides)]
    own[0] = after(own[0], *messages)

    def across(sums, axis_pairs):
        return lax.ppermute(sums, "pair", axis_pairs)

    mine, other, give, peak = own_pairs(own, orbitals)
    got = across(give, swap)
    top, to_half = scale_down(peak, got, 2 * count * depth)
    half = ((other + got[1, : 2 * domain]) * to_half[:1]).astype(F16)
    parts = [(mine, got[0, : 2 * domain], across(half, cross))]
    from_half = scale_up(across(top, cross), 2 * count * depth)
    here[0] = after(here[0], parts[0][2], from_half, row_vals)

    groups = [[(0, 0), (1, 0)], *GROUPS[0], *GROUPS[1]]
    sums = near_pairs(partners, own, here, near, orbitals, GROUPS[0])
    here[0] = after(here[0], sums[0])
    sums += near_pairs(partners, own, here, near, orbitals, GROUPS[1])
    for n in range(0, len(sums), 4):
        mine, other, give, give_on = sums[n : n + 4]
        if n:
            give_on = after(give_on, half)
        half = ((other + across(give_on, swap)) * to_half[:1]).astype(F16)
        got = across(give, swap)
        parts.append((mine, got, across(half, cross)))

    out = partners.shape + (domain, wide)
    amps, shares = [], []
    for at, (mine, got, arrived) in enumerate(parts):
        back = after(from_half, shares[-1]) if at else from_half
        total = mine + got + arrived.astype(F32) * back[:1]
        if at < len(parts) - 1:
            *amps, share = finish(total, row_vals, col_vals, groups[at], amps, out)
            shares.append(share)
    values, share = finish_last(total, row_vals, col_vals, groups[-1], groups[:-1], shares)
    others = [lax.ppermute(share, "pair", to) for to in (swap, cross, both)]
    return put(groups[-1], values, amps[0]), last([share, *others])


def padded(shard, sides, width):
    for axis, dim in sides:
        size, length = (lax.axis_size(axis), shard.shape[dim])
        up = [(i, (i + 1) % size) for i in range(size - 1)]
        down = [(j, i) for i, j in up]
        last = lax.slice_in_dim(shard, length - width, length, axis=dim)
        first = lax.slice_in_dim(shard, 0, width, axis=dim)
        before = lax.ppermute(last, axis, up)
        after = lax.ppermute(first, axis, down)
        shard = jnp.concatenate([before, shard, after], axis=dim)
    return shard


def general(half_ints, partners, domains, occ_energy, vir_energy):
    blocks_here, slots = partners.shape
    orbitals = half_ints.shape[2]
    domain = half_ints.shape[3]
    row_width = orbitals * domain
    first_block = lax.axis_index("aux") * blocks_here
    owned = lax.all_to_all(half_ints, "aux", split_axis=1, concat_axis=0, tiled=True)
    widened = padded(owned, (("aux", 1),), blocks_here)
    flat_rows = widened.reshape(widened.shape[0], 3 * blocks_here, row_width)
    own_blocks = flat_rows[:, blocks_here : 2 * blocks_here]
    positions = (partners - first_block + blocks_here).reshape(-1)
    partner_rows = jnp.take(flat_rows, positions, axis=1).reshape(
        flat_rows.shape[0], blocks_here, slots, row_width
    )
    partial_terms = jnp.einsum(
        "qlr,qlsc->lsrc", own_blocks, partner_rows, preferred_element_type=jnp.float32
    )
    my_sums = lax.psum_scatter(partial_terms, "pair", scatter_dimension=2, tiled=True)
    row_count = my_sums.shape[2]
    row_start = lax.axis_index("pair") * row_count
    block_ids = first_block + jnp.arange(blocks_here, dtype=jnp.int32)
    row_vals = (
        jnp.take(occ_energy, block_ids, axis=0)[:, :, None]
        - jnp.take(vir_energy, jnp.take(domains, block_ids, axis=0), axis=0)[:, None, :]
    )
    row_vals = lax.dynamic_slice_in_dim(
        row_vals.reshape(blocks_here, row_width), row_start, row_count, 1
    )
    col_vals = (
        jnp.take(occ_energy, partners, axis=0)[:, :, :, None]
        - jnp.take(vir_energy, jnp.take(domains, partners, axis=0), axis=0)[:, :, None, :]
    )
    col_vals = col_vals.reshape(blocks_here, slots, row_width)
    denominator = row_vals[:, None, :, None] + col_vals[:, :, None, :]
    amplitudes = my_sums / denominator
    weighted = (
        (my_sums * amplitudes).reshape(blocks_here, slots, row_count, orbitals, domain).sum(axis=4)
    )
    orbital_of = (row_start + jnp.arange(row_count, dtype=jnp.int32)) // domain
    selector = (orbital_of[:, None] == jnp.arange(orbitals, dtype=jnp.int32)[None, :]).astype(
        jnp.float32
    )
    partial_energy = jnp.einsum(
        "lskj,ki->lsij", weighted, selector, precision=lax.Precision.HIGHEST
    )
    pair_energy = lax.psum(partial_energy, "pair") / (domain * domain)
    return (amplitudes, pair_energy)


def on_device(half_ints, partners, domains, occ_energy, vir_energy):
    _, _, orbitals, domain = half_ints.shape
    fits = partners.shape[0] == 2 and domain == 128 and vir_energy.shape[0] % domain == 0
    fits &= lax.axis_size("pair") == lax.axis_size("aux") == orbitals == 4
    step = fast if fits and half_ints.shape[0] % 16 == 0 else general
    return step(half_ints, partners, domains, occ_energy, vir_energy)


def solution(mesh):
    return jax.shard_map(
        on_device,
        mesh=mesh,
        in_specs=(
            P(("frag", "aux", "pair"), None, None, None),
            P(("frag", "aux"), None),
            P("frag", None),
            P("frag", None),
            P("frag"),
        ),
        out_specs=(P(("frag", "aux"), None, "pair", None), P(("frag", "aux"), None, None, None)),
        check_vma=False,
    )
```

```python
import jax
import jax.numpy as jnp
from jax import lax
from jax.experimental import pallas as pl
from jax.experimental.pallas import tpu as pltpu
from jax.sharding import PartitionSpec as P

BF16, F16, F32 = jnp.bfloat16, jnp.float16, jnp.float32
VMEM = pl.BlockSpec(memory_space=pltpu.VMEM)
SMEM = pl.BlockSpec(memory_space=pltpu.SMEM)
ANY = pl.BlockSpec(memory_space=pl.ANY)
PARAMS = pltpu.CompilerParams(vmem_limit_bytes=8 * 2**20)
PEAK_ROWS = 16
GROUPS = ([[(0, 1)]], [[(1, 1), (0, 2), (1, 2)]])

def shape(*dims, dtype=F32):
    return jax.ShapeDtypeStruct(dims, dtype)


def call(kernel, name, **options):
    return pl.pallas_call(kernel, compiler_params=PARAMS, name=name, **options)


def after(value, *others):
    return lax.optimization_barrier((value, *others))[0]


def panel_at(depth, orbital, block):
    return pl.ds((orbital * 2 + block) * depth, depth)


def depth_of(one_set, orbitals):
    return (one_set.shape[0] - PEAK_ROWS) // (2 * orbitals)


def pack(raw, count):
    depth, blocks, orbitals, domain = raw.shape
    rows = blocks * orbitals
    group = rows // 2

    def kernel(raw_ref, *refs):
        outs, (narrow, wide, sems) = refs[:count], refs[count:]
        z = lax.axis_index("aux")
        copies = []
        for n in range(2):
            start = pl.multiple_of((lax.div(z, 2) ^ (1 - n)) * group, 16)
            part = raw_ref.at[:, pl.ds(start, group), :]
            copies.append(pltpu.make_async_copy(part, narrow.at[n], sems.at[n]))
            copies[-1].start()
        peak = jnp.zeros((PEAK_ROWS, domain), F32)
        for n, ks in enumerate(((2, 3), (0, 1))):
            copies[n].wait()
            values = narrow[n].astype(F32).reshape(depth * group, domain)
            wide[n] = values
            values = jnp.max(jnp.abs(values).reshape(-1, PEAK_ROWS, domain), axis=0)
            peak = jnp.maximum(peak, values)
            for k in ks:
                first = lax.rem(z ^ k, 2) * 2 * orbitals
                for r in range(2):
                    for i in range(orbitals):
                        at = pl.ds(first + r * orbitals + i, depth, stride=group)
                        outs[k][panel_at(depth, i, r), :] = wide[n, at, :].astype(BF16)
        for out in outs:
            out[2 * orbitals * depth :, :] = peak.astype(BF16)

    one_set = shape(2 * orbitals * depth + PEAK_ROWS, domain, dtype=BF16)
    return call(
        kernel,
        "pack",
        out_shape=[one_set] * count,
        in_specs=[pl.BlockSpec(memory_space=pltpu.HBM)],
        out_specs=[VMEM] * count,
        scratch_shapes=[
            pltpu.VMEM((2, depth, group, domain), BF16),
            pltpu.VMEM((2, depth * group, domain), F32),
            pltpu.SemaphoreType.DMA((2,)),
        ],
    )(pltpu.with_memory_space_constraint(raw.reshape(depth, rows, domain), pltpu.HBM))


def relay(own, rows):
    domain = own[0].shape[1]

    def kernel(*refs):
        own_refs, outs = refs[:4], refs[4:]
        for out, partner in zip(outs, (1, 3)):
            for k in (1, 2, 3):
                out[(k - 1) * rows : k * rows] = own_refs[k ^ partner][:rows]

    return call(
        kernel,
        "relay",
        out_shape=[shape(3 * rows, domain, dtype=BF16)] * 2,
        in_specs=[VMEM] * 4,
        out_specs=[VMEM] * 2,
    )(*own)


def product(left, right):
    return lax.dot_general(left, right, (((0,), (0,)), ((), ())), preferred_element_type=F32)


def left_rows(own_refs, depth, r):
    p = lax.axis_index("pair")
    x, c = p // 2, lax.rem(p, 2)
    order = (2 * x + c, 2 * (1 - x) + c, 2 * x + 1 - c, 2 * (1 - x) + 1 - c)
    columns = [
        jnp.concatenate([ref[panel_at(depth, i, r), :] for ref in own_refs], axis=0) for i in order
    ]
    return jnp.concatenate(columns, axis=1)


def store_sums(sums, at, *outs):
    domain = sums.shape[0] // 4
    for n, out in enumerate(outs):
        out[at] = sums[n * domain : (n + 1) * domain]


def own_pairs(own, orbitals):
    count, domain = len(own), own[0].shape[1]
    depth = depth_of(own[0], orbitals)
    wide = orbitals * domain

    def kernel(*refs):
        own_refs, (mine, other, give, peak) = refs[:count], refs[count:]
        top = own_refs[0][-PEAK_ROWS:, :].astype(F32)
        for ref in own_refs[1:]:
            top = jnp.maximum(top, ref[-PEAK_ROWS:, :].astype(F32))
        top = jnp.maximum(top[:8], top[8:])
        peak[...] = jnp.concatenate([top] * orbitals, axis=1)
        for n in range(2):
            give[n, 2 * domain :] = peak[...]
        for r in range(2):
            right = jnp.concatenate(
                [
                    jnp.concatenate([ref[panel_at(depth, j, r), :] for ref in own_refs], axis=0)
                    for j in range(orbitals)
                ],
                axis=1,
            )
            at = slice(r * domain, (r + 1) * domain)
            store_sums(product(left_rows(own_refs, depth, r), right), at, mine, other, give.at[0], give.at[1])

    return call(
        kernel,
        "own",
        out_shape=[
            shape(2 * domain, wide),
            shape(2 * domain, wide),
            shape(2, 2 * domain + 8, wide),
            shape(8, wide),
        ],
        in_specs=[VMEM] * count,
        out_specs=[VMEM] * 4,
    )(*own)


def near_pairs(partners, own, here, sides, orbitals, groups):
    count, domain = len(own), own[0].shape[1]
    depth = depth_of(own[0], orbitals)
    rows, wide = 2 * orbitals * depth, orbitals * domain

    def kernel(partners_ref, *refs):
        own_refs, here_refs, side_refs = refs[:count], refs[count : count + 2], refs[count + 2 :][:2]
        outs = refs[count + 4 :]
        z = lax.axis_index("aux")

        def flag(value):
            return jnp.broadcast_to(value, (depth, domain))

        def panels(r, j, slot, w):
            from_first = flag(jnp.where(w > 3, 1, 0) != lax.rem(z, 2))
            is_own, is_second = flag((w == 2) | (w == 3)), flag(lax.rem(w, 2) == 1)

            def either(first, second, start):
                rows_at = slice(start, start + depth)
                return jnp.where(from_first, first[rows_at, :], second[rows_at, :])

            found = []
            for k in range(count):
                refs, start = (here_refs, 0) if k == 0 else (side_refs, (k - 1) * rows)
                start += 2 * j * depth
                if slot == 1:
                    panel = either(*refs, start + r * depth)
                else:
                    panel = jnp.where(is_second, either(*refs, start + depth), either(*refs, start))
                    mine = [own_refs[k][panel_at(depth, j, block), :] for block in range(2)]
                    panel = jnp.where(is_own, jnp.where(is_second, mine[1], mine[0]), panel)
                found.append(panel)
            return jnp.concatenate(found, axis=0)

        for n, tiles in enumerate(groups):
            for t, (r, slot) in enumerate(tiles):
                w = partners_ref[r : r + 1, slot : slot + 1] - 2 * z + 2
                right = jnp.concatenate([panels(r, j, slot, w) for j in range(orbitals)], axis=1)
                sums = product(left_rows(own_refs, depth, r), right)
                at = slice(t * domain, (t + 1) * domain)
                store_sums(sums, at, *outs[4 * n : 4 * n + 4])

    shapes = []
    for tiles in groups:
        shapes += [shape(len(tiles) * domain, wide)] * 4
    return call(
        kernel,
        "near",
        out_shape=shapes,
        in_specs=[VMEM] * (count + 5),
        out_specs=[VMEM] * len(shapes),
    )(partners, *own, *here, *sides)


def scale_down(peak, got, depth):
    def kernel(peak_ref, got_ref, top_ref, down_ref):
        top = jnp.maximum(peak_ref[...], got_ref[0, -8:])
        top_ref[...] = top
        top = jnp.maximum(jnp.max(top[:, :128], axis=(0, 1), keepdims=True), 1e-17)
        down_ref[...] = jnp.broadcast_to(32768.0 / (top * top * depth), down_ref.shape)

    return call(
        kernel,
        "scale_down",
        out_shape=[shape(*peak.shape)] * 2,
        in_specs=[VMEM] * 2,
        out_specs=[VMEM] * 2,
    )(peak, got)


def scale_up(top, depth):
    def kernel(top_ref, up_ref):
        top = jnp.maximum(jnp.max(top_ref[:, :128], axis=(0, 1), keepdims=True), 1e-17)
        up_ref[...] = jnp.broadcast_to((top * top * depth) * (1.0 / 32768.0), up_ref.shape)

    return call(
        kernel, "scale_up", out_shape=shape(*top.shape), in_specs=[VMEM], out_specs=VMEM
    )(top)


def amplitude_tiles(total_ref, row_ref, col_ref, amp, energy_ref, tiles, done):
    rows, wide = amp.shape[1:]
    for t, (r, slot) in enumerate(tiles):
        row = row_ref[r]
        for j in range(wide // rows):
            at = slice(j * rows, (j + 1) * rows)
            total = total_ref[t * rows : (t + 1) * rows, at]
            tile = total / (row + col_ref[r, slot, j : j + 1, :])
            amp[t, :, at] = tile
            energy_ref[t, j : j + 1, :] = jnp.sum(total * tile, axis=0, keepdims=True)
        done(t)


def finish(totals, row_vals, col_vals, tiles, before, out):
    rows, wide = out[2:]
    count = len(tiles)

    def kernel(total_ref, row_ref, col_ref, *refs):
        amp_ref, energy_ref, amp, sems = refs[-4:]
        copies = []

        def done(t):
            r, slot = tiles[t]
            copies.append(pltpu.make_async_copy(amp.at[t], amp_ref.at[r, slot], sems.at[t]))
            copies[-1].start()

        amplitude_tiles(total_ref, row_ref, col_ref, amp, energy_ref, tiles, done)
        for started in copies:
            started.wait()

    return call(
        kernel,
        "finish",
        out_shape=[shape(*out), shape(count, wide // rows, rows)],
        in_specs=[VMEM] * 3 + [ANY] * len(before),
        out_specs=[ANY, VMEM],
        input_output_aliases={3: 0} if before else {},
        scratch_shapes=[pltpu.VMEM((count, rows, wide), F32), pltpu.SemaphoreType.DMA((count,))],
    )(totals, row_vals, col_vals, *before)


def finish_last(totals, row_vals, col_vals, tiles, before, shares):
    orbitals, domain = col_vals.shape[2:]
    wide = orbitals * domain
    blocks, slots = col_vals.shape[:2]
    count = len(tiles)
    known = len(shares)

    def kernel(total_ref, row_ref, col_ref, *refs):
        share_refs, (amp_ref, out, energy) = refs[:known], refs[known:]
        amplitude_tiles(total_ref, row_ref, col_ref, amp_ref, energy, tiles, lambda t: None)
        p = lax.axis_index("pair")
        row = lax.broadcasted_iota(jnp.int32, (orbitals, orbitals), 0)
        column = lax.broadcasted_iota(jnp.int32, (orbitals, orbitals), 1)
        for ref, places in zip((*share_refs, energy), (*before, tiles)):
            for t, (r, slot) in enumerate(places):
                sums = jnp.sum(ref[t], axis=1, keepdims=True) * (1.0 / (domain * domain))
                value = jnp.zeros((orbitals, orbitals), F32)
                for j in range(orbitals):
                    value = jnp.where((row == p) & (column == j), sums[j : j + 1, :], value)
                out[r, slot] = value

    return call(
        kernel,
        "finish_last",
        out_shape=[shape(count, domain, wide), shape(blocks, slots, orbitals, orbitals)],
        in_specs=[VMEM] * (3 + known),
        out_specs=[VMEM] * 2,
        scratch_shapes=[pltpu.VMEM((count, orbitals, domain), F32)],
    )(totals, row_vals, col_vals, *shares)


def put(tiles_at, values, amps):
    def kernel(values_ref, _, amp_ref, sems):
        copies = []
        for t, (r, slot) in enumerate(tiles_at):
            copies.append(pltpu.make_async_copy(values_ref.at[t], amp_ref.at[r, slot], sems.at[t]))
            copies[-1].start()
        for started in copies:
            started.wait()

    return call(
        kernel,
        "put",
        out_shape=shape(*amps.shape),
        in_specs=[VMEM, ANY],
        out_specs=ANY,
        input_output_aliases={1: 0},
        scratch_shapes=[pltpu.SemaphoreType.DMA((len(tiles_at),))],
    )(values, amps)


def last(shares):
    def kernel(*refs):
        refs[4][...] = (refs[0][...] + refs[1][...]) + (refs[2][...] + refs[3][...])

    return call(
        kernel,
        "last",
        out_shape=shape(*shares[0].shape),
        in_specs=[VMEM] * 4,
        out_specs=VMEM,
    )(*shares)


def energies(partners, domains, occ_energy, vir_energy):
    blocks, domain = domains.shape
    orbitals = occ_energy.shape[1]
    here, slots = partners.shape
    tables = vir_energy.shape[0] // domain

    def kernel(partners_ref, occ_ref, domains_ref, vir_ref, row_ref, col_ref, picked):
        at = domains_ref[...]
        lane, table = lax.rem(at, domain), lax.div(at, domain)
        vir = jnp.zeros(at.shape, F32)
        for t in range(tables):
            values = jnp.broadcast_to(vir_ref[t : t + 1, :], at.shape)
            vir = jnp.where(table == t, jnp.take_along_axis(values, lane, axis=1), vir)
        picked[...] = vir
        z, p = lax.axis_index("aux"), lax.axis_index("pair")
        for r in range(here):
            block = here * z + r
            value = occ_ref[p, block] - picked[pl.ds(block, 1), :]
            row_ref[r] = jnp.broadcast_to(value, (domain, domain)).T
            for s in range(slots):
                other = partners_ref[r, s]
                value = picked[pl.ds(other, 1), :]
                for j in range(orbitals):
                    col_ref[r, s, j : j + 1, :] = occ_ref[j, other] - value

    return call(
        kernel,
        "energies",
        out_shape=[shape(here, domain, domain), shape(here, slots, orbitals, domain)],
        in_specs=[SMEM] * 2 + [VMEM] * 2,
        out_specs=[VMEM] * 2,
        scratch_shapes=[pltpu.VMEM((blocks, domain), F32)],
    )(partners, occ_energy.T, domains, vir_energy.reshape(tables, domain))


def fast(half_ints, partners, domains, occ_energy, vir_energy):
    depth, _, orbitals, domain = half_ints.shape
    count = lax.axis_size("aux")
    wide = orbitals * domain
    sides = [[(i, i ^ 4) for i in range(16)], [(i, i ^ (12 if 4 <= i < 12 else 1)) for i in range(16)]]
    swap, cross, both = ([(i, i ^ k) for i in range(4)] for k in (1, 2, 3))

    own_here, *sends = pack(half_ints, count)
    here = [sends[0], sends[2]]
    own = [own_here]
    for k, send in enumerate(sends, 1):
        own.append(lax.ppermute(send, "aux", [(i, i ^ k) for i in range(count)]))
    row_vals, col_vals = energies(partners, domains, occ_energy, vir_energy)
    messages = relay(own, 2 * orbitals * depth)
    near = [lax.ppermute(m, ("aux", "pair"), side) for m, side in zip(messages, sides)]
    own[0] = after(own[0], *messages)

    def across(sums, axis_pairs):
        return lax.ppermute(sums, "pair", axis_pairs)

    mine, other, give, peak = own_pairs(own, orbitals)
    got = across(give, swap)
    top, to_half = scale_down(peak, got, 2 * count * depth)
    half = ((other + got[1, : 2 * domain]) * to_half[:1]).astype(F16)
    parts = [(mine, got[0, : 2 * domain], across(half, cross))]
    from_half = scale_up(across(top, cross), 2 * count * depth)
    here[0] = after(here[0], parts[0][2], from_half, row_vals)

    groups = [[(0, 0), (1, 0)], *GROUPS[0], *GROUPS[1]]
    sums = near_pairs(partners, own, here, near, orbitals, GROUPS[0])
    here[0] = after(here[0], sums[0])
    sums += near_pairs(partners, own, here, near, orbitals, GROUPS[1])
    mine_a, other_a, give_a, on_a, mine_b, other_b, give_b, on_b = sums
    half_a = ((other_a + across(on_a, swap)) * to_half[:1]).astype(F16)
    x_a = across(half_a, cross)
    on_b = after(on_b, half_a)
    half_b = ((other_b + across(on_b, swap)) * to_half[:1]).astype(F16)
    x_b = across(half_b, cross)
    parts.append((mine_a, across(after(give_a, half_a), swap), x_a))
    parts.append((mine_b, across(after(give_b, half_a), swap), x_b))

    out = partners.shape + (domain, wide)
    amps, shares = [], []
    for at, (mine, got, arrived) in enumerate(parts):
        back = after(from_half, shares[-1]) if at else from_half
        total = mine + got + arrived.astype(F32) * back[:1]
        if at < len(parts) - 1:
            *amps, share = finish(total, row_vals, col_vals, groups[at], amps, out)
            shares.append(share)
    values, share = finish_last(total, row_vals, col_vals, groups[-1], groups[:-1], shares)
    others = [lax.ppermute(share, "pair", to) for to in (swap, cross, both)]
    return put(groups[-1], values, amps[0]), last([share, *others])


def padded(shard, sides, width):
    for axis, dim in sides:
        size, length = (lax.axis_size(axis), shard.shape[dim])
        up = [(i, (i + 1) % size) for i in range(size - 1)]
        down = [(j, i) for i, j in up]
        last = lax.slice_in_dim(shard, length - width, length, axis=dim)
        first = lax.slice_in_dim(shard, 0, width, axis=dim)
        before = lax.ppermute(last, axis, up)
        after = lax.ppermute(first, axis, down)
        shard = jnp.concatenate([before, shard, after], axis=dim)
    return shard


def general(half_ints, partners, domains, occ_energy, vir_energy):
    blocks_here, slots = partners.shape
    orbitals = half_ints.shape[2]
    domain = half_ints.shape[3]
    row_width = orbitals * domain
    first_block = lax.axis_index("aux") * blocks_here
    owned = lax.all_to_all(half_ints, "aux", split_axis=1, concat_axis=0, tiled=True)
    widened = padded(owned, (("aux", 1),), blocks_here)
    flat_rows = widened.reshape(widened.shape[0], 3 * blocks_here, row_width)
    own_blocks = flat_rows[:, blocks_here : 2 * blocks_here]
    positions = (partners - first_block + blocks_here).reshape(-1)
    partner_rows = jnp.take(flat_rows, positions, axis=1).reshape(
        flat_rows.shape[0], blocks_here, slots, row_width
    )
    partial_terms = jnp.einsum(
        "qlr,qlsc->lsrc", own_blocks, partner_rows, preferred_element_type=jnp.float32
    )
    my_sums = lax.psum_scatter(partial_terms, "pair", scatter_dimension=2, tiled=True)
    row_count = my_sums.shape[2]
    row_start = lax.axis_index("pair") * row_count
    block_ids = first_block + jnp.arange(blocks_here, dtype=jnp.int32)
    row_vals = (
        jnp.take(occ_energy, block_ids, axis=0)[:, :, None]
        - jnp.take(vir_energy, jnp.take(domains, block_ids, axis=0), axis=0)[:, None, :]
    )
    row_vals = lax.dynamic_slice_in_dim(
        row_vals.reshape(blocks_here, row_width), row_start, row_count, 1
    )
    col_vals = (
        jnp.take(occ_energy, partners, axis=0)[:, :, :, None]
        - jnp.take(vir_energy, jnp.take(domains, partners, axis=0), axis=0)[:, :, None, :]
    )
    col_vals = col_vals.reshape(blocks_here, slots, row_width)
    denominator = row_vals[:, None, :, None] + col_vals[:, :, None, :]
    amplitudes = my_sums / denominator
    weighted = (
        (my_sums * amplitudes).reshape(blocks_here, slots, row_count, orbitals, domain).sum(axis=4)
    )
    orbital_of = (row_start + jnp.arange(row_count, dtype=jnp.int32)) // domain
    selector = (orbital_of[:, None] == jnp.arange(orbitals, dtype=jnp.int32)[None, :]).astype(
        jnp.float32
    )
    partial_energy = jnp.einsum(
        "lskj,ki->lsij", weighted, selector, precision=lax.Precision.HIGHEST
    )
    pair_energy = lax.psum(partial_energy, "pair") / (domain * domain)
    return (amplitudes, pair_energy)


def on_device(half_ints, partners, domains, occ_energy, vir_energy):
    _, _, orbitals, domain = half_ints.shape
    fits = partners.shape[0] == 2 and domain == 128 and vir_energy.shape[0] % domain == 0
    fits &= lax.axis_size("pair") == lax.axis_size("aux") == orbitals == 4
    step = fast if fits and half_ints.shape[0] % 16 == 0 else general
    return step(half_ints, partners, domains, occ_energy, vir_energy)


def solution(mesh):
    return jax.shard_map(
        on_device,
        mesh=mesh,
        in_specs=(
            P(("frag", "aux", "pair"), None, None, None),
            P(("frag", "aux"), None),
            P("frag", None),
            P("frag", None),
            P("frag"),
        ),
        out_specs=(P(("frag", "aux"), None, "pair", None), P(("frag", "aux"), None, None, None)),
        check_vma=False,
    )
```

```python
import jax
import jax.numpy as jnp
from jax import lax
from jax.experimental import pallas as pl
from jax.experimental.pallas import tpu as pltpu
from jax.sharding import PartitionSpec as P

BF16, F16, F32 = jnp.bfloat16, jnp.float16, jnp.float32
VMEM = pl.BlockSpec(memory_space=pltpu.VMEM)
SMEM = pl.BlockSpec(memory_space=pltpu.SMEM)
ANY = pl.BlockSpec(memory_space=pl.ANY)
PARAMS = pltpu.CompilerParams(vmem_limit_bytes=8 * 2**20)
PEAK_ROWS = 16
GROUPS = ([[(0, 1)]], [[(1, 1), (0, 2), (1, 2)]])

def shape(*dims, dtype=F32):
    return jax.ShapeDtypeStruct(dims, dtype)


def call(kernel, name, **options):
    return pl.pallas_call(kernel, compiler_params=PARAMS, name=name, **options)


def after(value, *others):
    return lax.optimization_barrier((value, *others))[0]


def panel_at(depth, orbital, block):
    return pl.ds((orbital * 2 + block) * depth, depth)


def depth_of(one_set, orbitals):
    return (one_set.shape[0] - PEAK_ROWS) // (2 * orbitals)


def pack(raw, count):
    depth, blocks, orbitals, domain = raw.shape
    rows = blocks * orbitals
    group = rows // 2

    def kernel(raw_ref, *refs):
        outs, (narrow, wide, sems) = refs[:count], refs[count:]
        z = lax.axis_index("aux")
        copies = []
        for n in range(2):
            start = pl.multiple_of((lax.div(z, 2) ^ (1 - n)) * group, 16)
            part = raw_ref.at[:, pl.ds(start, group), :]
            copies.append(pltpu.make_async_copy(part, narrow.at[n], sems.at[n]))
            copies[-1].start()
        peak = jnp.zeros((PEAK_ROWS, domain), F32)
        for n, ks in enumerate(((2, 3), (0, 1))):
            copies[n].wait()
            values = narrow[n].astype(F32).reshape(depth * group, domain)
            wide[n] = values
            values = jnp.max(jnp.abs(values).reshape(-1, PEAK_ROWS, domain), axis=0)
            peak = jnp.maximum(peak, values)
            for k in ks:
                first = lax.rem(z ^ k, 2) * 2 * orbitals
                for r in range(2):
                    for i in range(orbitals):
                        at = pl.ds(first + r * orbitals + i, depth, stride=group)
                        outs[k][panel_at(depth, i, r), :] = wide[n, at, :].astype(BF16)
        for out in outs:
            out[2 * orbitals * depth :, :] = peak.astype(BF16)

    one_set = shape(2 * orbitals * depth + PEAK_ROWS, domain, dtype=BF16)
    return call(
        kernel,
        "pack",
        out_shape=[one_set] * count,
        in_specs=[pl.BlockSpec(memory_space=pltpu.HBM)],
        out_specs=[VMEM] * count,
        scratch_shapes=[
            pltpu.VMEM((2, depth, group, domain), BF16),
            pltpu.VMEM((2, depth * group, domain), F32),
            pltpu.SemaphoreType.DMA((2,)),
        ],
    )(pltpu.with_memory_space_constraint(raw.reshape(depth, rows, domain), pltpu.HBM))


def relay(own, rows):
    domain = own[0].shape[1]

    def kernel(*refs):
        own_refs, outs = refs[:4], refs[4:]
        for out, partner in zip(outs, (1, 3)):
            for k in (1, 2, 3):
                out[(k - 1) * rows : k * rows] = own_refs[k ^ partner][:rows]

    return call(
        kernel,
        "relay",
        out_shape=[shape(3 * rows, domain, dtype=BF16)] * 2,
        in_specs=[VMEM] * 4,
        out_specs=[VMEM] * 2,
    )(*own)


def product(left, right):
    return lax.dot_general(left, right, (((0,), (0,)), ((), ())), preferred_element_type=F32)


def left_rows(own_refs, depth, r, part=slice(0, 4)):
    p = lax.axis_index("pair")
    x, c = p // 2, lax.rem(p, 2)
    order = (2 * x + c, 2 * (1 - x) + c, 2 * x + 1 - c, 2 * (1 - x) + 1 - c)
    columns = [
        jnp.concatenate([ref[panel_at(depth, i, r), :] for ref in own_refs], axis=0) for i in order[part]
    ]
    return jnp.concatenate(columns, axis=1)


def store_sums(sums, at, *outs):
    domain = sums.shape[0] // 4
    for n, out in enumerate(outs):
        out[at] = sums[n * domain : (n + 1) * domain]


def own_right(own_refs, depth, r, orbitals):
    columns = [
        jnp.concatenate([ref[panel_at(depth, j, r), :] for ref in own_refs], axis=0)
        for j in range(orbitals)
    ]
    return jnp.concatenate(columns, axis=1)


def own_pairs(own, orbitals, given):
    count, domain = len(own), own[0].shape[1]
    depth = depth_of(own[0], orbitals)
    wide = orbitals * domain
    part = slice(2, 4) if given else slice(0, 2)

    def kernel(*refs):
        own_refs, outs = refs[:count], refs[count:]
        if given:
            give, peak = outs
            top = own_refs[0][-PEAK_ROWS:, :].astype(F32)
            for ref in own_refs[1:]:
                top = jnp.maximum(top, ref[-PEAK_ROWS:, :].astype(F32))
            top = jnp.maximum(top[:8], top[8:])
            peak[...] = jnp.concatenate([top] * orbitals, axis=1)
            for n in range(2):
                give[n, 2 * domain :] = peak[...]
            outs = (give.at[0], give.at[1])
        for r in range(2):
            left = left_rows(own_refs, depth, r, part)
            sums = product(left, own_right(own_refs, depth, r, orbitals))
            at = slice(r * domain, (r + 1) * domain)
            outs[0][at], outs[1][at] = sums[:domain], sums[domain:]

    kept = [shape(2 * domain, wide)] * 2
    return call(
        kernel,
        "own_give" if given else "own_keep",
        out_shape=[shape(2, 2 * domain + 8, wide), shape(8, wide)] if given else kept,
        in_specs=[VMEM] * count,
        out_specs=[VMEM] * 2,
    )(*own)


def near_pairs(partners, own, here, sides, orbitals, groups):
    count, domain = len(own), own[0].shape[1]
    depth = depth_of(own[0], orbitals)
    rows, wide = 2 * orbitals * depth, orbitals * domain

    def kernel(partners_ref, *refs):
        own_refs, here_refs, side_refs = refs[:count], refs[count : count + 2], refs[count + 2 :][:2]
        outs = refs[count + 4 :]
        z = lax.axis_index("aux")

        def flag(value):
            return jnp.broadcast_to(value, (depth, domain))

        def panels(r, j, slot, w):
            from_first = flag(jnp.where(w > 3, 1, 0) != lax.rem(z, 2))
            is_own, is_second = flag((w == 2) | (w == 3)), flag(lax.rem(w, 2) == 1)

            def either(first, second, start):
                rows_at = slice(start, start + depth)
                return jnp.where(from_first, first[rows_at, :], second[rows_at, :])

            found = []
            for k in range(count):
                refs, start = (here_refs, 0) if k == 0 else (side_refs, (k - 1) * rows)
                start += 2 * j * depth
                if slot == 1:
                    panel = either(*refs, start + r * depth)
                else:
                    panel = jnp.where(is_second, either(*refs, start + depth), either(*refs, start))
                    mine = [own_refs[k][panel_at(depth, j, block), :] for block in range(2)]
                    panel = jnp.where(is_own, jnp.where(is_second, mine[1], mine[0]), panel)
                found.append(panel)
            return jnp.concatenate(found, axis=0)

        for n, tiles in enumerate(groups):
            for t, (r, slot) in enumerate(tiles):
                w = partners_ref[r : r + 1, slot : slot + 1] - 2 * z + 2
                right = jnp.concatenate([panels(r, j, slot, w) for j in range(orbitals)], axis=1)
                sums = product(left_rows(own_refs, depth, r), right)
                at = slice(t * domain, (t + 1) * domain)
                store_sums(sums, at, *outs[4 * n : 4 * n + 4])

    shapes = []
    for tiles in groups:
        shapes += [shape(len(tiles) * domain, wide)] * 4
    return call(
        kernel,
        "near",
        out_shape=shapes,
        in_specs=[VMEM] * (count + 5),
        out_specs=[VMEM] * len(shapes),
    )(partners, *own, *here, *sides)


def scale_down(peak, got, depth):
    def kernel(peak_ref, got_ref, top_ref, down_ref):
        top = jnp.maximum(peak_ref[...], got_ref[0, -8:])
        top_ref[...] = top
        top = jnp.maximum(jnp.max(top[:, :128], axis=(0, 1), keepdims=True), 1e-17)
        down_ref[...] = jnp.broadcast_to(32768.0 / (top * top * depth), down_ref.shape)

    return call(
        kernel,
        "scale_down",
        out_shape=[shape(*peak.shape)] * 2,
        in_specs=[VMEM] * 2,
        out_specs=[VMEM] * 2,
    )(peak, got)


def scale_up(top, depth):
    def kernel(top_ref, up_ref):
        top = jnp.maximum(jnp.max(top_ref[:, :128], axis=(0, 1), keepdims=True), 1e-17)
        up_ref[...] = jnp.broadcast_to((top * top * depth) * (1.0 / 32768.0), up_ref.shape)

    return call(
        kernel, "scale_up", out_shape=shape(*top.shape), in_specs=[VMEM], out_specs=VMEM
    )(top)


def amplitude_tiles(total_ref, row_ref, col_ref, amp, energy_ref, tiles, done):
    rows, wide = amp.shape[1:]
    for t, (r, slot) in enumerate(tiles):
        row = row_ref[r]
        for j in range(wide // rows):
            at = slice(j * rows, (j + 1) * rows)
            total = total_ref[t * rows : (t + 1) * rows, at]
            tile = total / (row + col_ref[r, slot, j : j + 1, :])
            amp[t, :, at] = tile
            energy_ref[t, j : j + 1, :] = jnp.sum(total * tile, axis=0, keepdims=True)
        done(t)


def finish(totals, row_vals, col_vals, tiles, before, out):
    rows, wide = out[2:]
    count = len(tiles)

    def kernel(total_ref, row_ref, col_ref, *refs):
        amp_ref, energy_ref, amp, sems = refs[-4:]
        copies = []

        def done(t):
            r, slot = tiles[t]
            copies.append(pltpu.make_async_copy(amp.at[t], amp_ref.at[r, slot], sems.at[t]))
            copies[-1].start()

        amplitude_tiles(total_ref, row_ref, col_ref, amp, energy_ref, tiles, done)
        for started in copies:
            started.wait()

    return call(
        kernel,
        "finish",
        out_shape=[shape(*out), shape(count, wide // rows, rows)],
        in_specs=[VMEM] * 3 + [ANY] * len(before),
        out_specs=[ANY, VMEM],
        input_output_aliases={3: 0} if before else {},
        scratch_shapes=[pltpu.VMEM((count, rows, wide), F32), pltpu.SemaphoreType.DMA((count,))],
    )(totals, row_vals, col_vals, *before)


def finish_last(totals, row_vals, col_vals, tiles, before, shares):
    orbitals, domain = col_vals.shape[2:]
    wide = orbitals * domain
    blocks, slots = col_vals.shape[:2]
    count = len(tiles)
    known = len(shares)

    def kernel(total_ref, row_ref, col_ref, *refs):
        share_refs, (amp_ref, out, energy) = refs[:known], refs[known:]
        amplitude_tiles(total_ref, row_ref, col_ref, amp_ref, energy, tiles, lambda t: None)
        p = lax.axis_index("pair")
        row = lax.broadcasted_iota(jnp.int32, (orbitals, orbitals), 0)
        column = lax.broadcasted_iota(jnp.int32, (orbitals, orbitals), 1)
        for ref, places in zip((*share_refs, energy), (*before, tiles)):
            for t, (r, slot) in enumerate(places):
                sums = jnp.sum(ref[t], axis=1, keepdims=True) * (1.0 / (domain * domain))
                value = jnp.zeros((orbitals, orbitals), F32)
                for j in range(orbitals):
                    value = jnp.where((row == p) & (column == j), sums[j : j + 1, :], value)
                out[r, slot] = value

    return call(
        kernel,
        "finish_last",
        out_shape=[shape(count, domain, wide), shape(blocks, slots, orbitals, orbitals)],
        in_specs=[VMEM] * (3 + known),
        out_specs=[VMEM] * 2,
        scratch_shapes=[pltpu.VMEM((count, orbitals, domain), F32)],
    )(totals, row_vals, col_vals, *shares)


def put(tiles_at, values, amps):
    def kernel(values_ref, _, amp_ref, sems):
        copies = []
        for t, (r, slot) in enumerate(tiles_at):
            copies.append(pltpu.make_async_copy(values_ref.at[t], amp_ref.at[r, slot], sems.at[t]))
            copies[-1].start()
        for started in copies:
            started.wait()

    return call(
        kernel,
        "put",
        out_shape=shape(*amps.shape),
        in_specs=[VMEM, ANY],
        out_specs=ANY,
        input_output_aliases={1: 0},
        scratch_shapes=[pltpu.SemaphoreType.DMA((len(tiles_at),))],
    )(values, amps)


def last(shares):
    def kernel(*refs):
        refs[4][...] = (refs[0][...] + refs[1][...]) + (refs[2][...] + refs[3][...])

    return call(
        kernel,
        "last",
        out_shape=shape(*shares[0].shape),
        in_specs=[VMEM] * 4,
        out_specs=VMEM,
    )(*shares)


def energies(partners, domains, occ_energy, vir_energy):
    blocks, domain = domains.shape
    orbitals = occ_energy.shape[1]
    here, slots = partners.shape
    tables = vir_energy.shape[0] // domain

    def kernel(partners_ref, occ_ref, domains_ref, vir_ref, row_ref, col_ref, picked):
        at = domains_ref[...]
        lane, table = lax.rem(at, domain), lax.div(at, domain)
        vir = jnp.zeros(at.shape, F32)
        for t in range(tables):
            values = jnp.broadcast_to(vir_ref[t : t + 1, :], at.shape)
            vir = jnp.where(table == t, jnp.take_along_axis(values, lane, axis=1), vir)
        picked[...] = vir
        z, p = lax.axis_index("aux"), lax.axis_index("pair")
        for r in range(here):
            block = here * z + r
            value = occ_ref[p, block] - picked[pl.ds(block, 1), :]
            row_ref[r] = jnp.broadcast_to(value, (domain, domain)).T
            for s in range(slots):
                other = partners_ref[r, s]
                value = picked[pl.ds(other, 1), :]
                for j in range(orbitals):
                    col_ref[r, s, j : j + 1, :] = occ_ref[j, other] - value

    return call(
        kernel,
        "energies",
        out_shape=[shape(here, domain, domain), shape(here, slots, orbitals, domain)],
        in_specs=[SMEM] * 2 + [VMEM] * 2,
        out_specs=[VMEM] * 2,
        scratch_shapes=[pltpu.VMEM((blocks, domain), F32)],
    )(partners, occ_energy.T, domains, vir_energy.reshape(tables, domain))


def fast(half_ints, partners, domains, occ_energy, vir_energy):
    depth, _, orbitals, domain = half_ints.shape
    count = lax.axis_size("aux")
    wide = orbitals * domain
    sides = [[(i, i ^ 4) for i in range(16)], [(i, i ^ (12 if 4 <= i < 12 else 1)) for i in range(16)]]
    swap, cross, both = ([(i, i ^ k) for i in range(4)] for k in (1, 2, 3))

    own_here, *sends = pack(half_ints, count)
    here = [sends[0], sends[2]]
    own = [own_here]
    for k, send in enumerate(sends, 1):
        own.append(lax.ppermute(send, "aux", [(i, i ^ k) for i in range(count)]))
    row_vals, col_vals = energies(partners, domains, occ_energy, vir_energy)
    messages = relay(own, 2 * orbitals * depth)
    near = [lax.ppermute(m, ("aux", "pair"), side) for m, side in zip(messages, sides)]
    own[0] = after(own[0], *messages)

    def across(sums, axis_pairs):
        return lax.ppermute(sums, "pair", axis_pairs)

    give, peak = own_pairs(own, orbitals, True)
    mine, other = own_pairs(own, orbitals, False)
    got = across(give, swap)
    top, to_half = scale_down(peak, got, 2 * count * depth)
    half = ((other + got[1, : 2 * domain]) * to_half[:1]).astype(F16)
    parts = [(mine, got[0, : 2 * domain], across(half, cross))]
    from_half = scale_up(across(top, cross), 2 * count * depth)
    here[0] = after(here[0], parts[0][2], from_half, row_vals)

    groups = [[(0, 0), (1, 0)], *GROUPS[0], *GROUPS[1]]
    sums = near_pairs(partners, own, here, near, orbitals, GROUPS[0])
    here[0] = after(here[0], sums[0])
    sums += near_pairs(partners, own, here, near, orbitals, GROUPS[1])
    mine_a, other_a, give_a, on_a, mine_b, other_b, give_b, on_b = sums
    half_a = ((other_a + across(on_a, swap)) * to_half[:1]).astype(F16)
    x_a = across(half_a, cross)
    on_b = after(on_b, half_a)
    half_b = ((other_b + across(on_b, swap)) * to_half[:1]).astype(F16)
    x_b = across(half_b, cross)
    parts.append((mine_a, across(after(give_a, half_a), swap), x_a))
    parts.append((mine_b, across(after(give_b, half_a), swap), x_b))

    out = partners.shape + (domain, wide)
    amps, shares = [], []
    for at, (mine, got, arrived) in enumerate(parts):
        back = after(from_half, shares[-1]) if at else from_half
        total = mine + got + arrived.astype(F32) * back[:1]
        if at < len(parts) - 1:
            *amps, share = finish(total, row_vals, col_vals, groups[at], amps, out)
            shares.append(share)
    values, share = finish_last(total, row_vals, col_vals, groups[-1], groups[:-1], shares)
    others = [lax.ppermute(share, "pair", to) for to in (swap, cross, both)]
    return put(groups[-1], values, amps[0]), last([share, *others])


def padded(shard, sides, width):
    for axis, dim in sides:
        size, length = (lax.axis_size(axis), shard.shape[dim])
        up = [(i, (i + 1) % size) for i in range(size - 1)]
        down = [(j, i) for i, j in up]
        last = lax.slice_in_dim(shard, length - width, length, axis=dim)
        first = lax.slice_in_dim(shard, 0, width, axis=dim)
        before = lax.ppermute(last, axis, up)
        after = lax.ppermute(first, axis, down)
        shard = jnp.concatenate([before, shard, after], axis=dim)
    return shard


def general(half_ints, partners, domains, occ_energy, vir_energy):
    blocks_here, slots = partners.shape
    orbitals = half_ints.shape[2]
    domain = half_ints.shape[3]
    row_width = orbitals * domain
    first_block = lax.axis_index("aux") * blocks_here
    owned = lax.all_to_all(half_ints, "aux", split_axis=1, concat_axis=0, tiled=True)
    widened = padded(owned, (("aux", 1),), blocks_here)
    flat_rows = widened.reshape(widened.shape[0], 3 * blocks_here, row_width)
    own_blocks = flat_rows[:, blocks_here : 2 * blocks_here]
    positions = (partners - first_block + blocks_here).reshape(-1)
    partner_rows = jnp.take(flat_rows, positions, axis=1).reshape(
        flat_rows.shape[0], blocks_here, slots, row_width
    )
    partial_terms = jnp.einsum(
        "qlr,qlsc->lsrc", own_blocks, partner_rows, preferred_element_type=jnp.float32
    )
    my_sums = lax.psum_scatter(partial_terms, "pair", scatter_dimension=2, tiled=True)
    row_count = my_sums.shape[2]
    row_start = lax.axis_index("pair") * row_count
    block_ids = first_block + jnp.arange(blocks_here, dtype=jnp.int32)
    row_vals = (
        jnp.take(occ_energy, block_ids, axis=0)[:, :, None]
        - jnp.take(vir_energy, jnp.take(domains, block_ids, axis=0), axis=0)[:, None, :]
    )
    row_vals = lax.dynamic_slice_in_dim(
        row_vals.reshape(blocks_here, row_width), row_start, row_count, 1
    )
    col_vals = (
        jnp.take(occ_energy, partners, axis=0)[:, :, :, None]
        - jnp.take(vir_energy, jnp.take(domains, partners, axis=0), axis=0)[:, :, None, :]
    )
    col_vals = col_vals.reshape(blocks_here, slots, row_width)
    denominator = row_vals[:, None, :, None] + col_vals[:, :, None, :]
    amplitudes = my_sums / denominator
    weighted = (
        (my_sums * amplitudes).reshape(blocks_here, slots, row_count, orbitals, domain).sum(axis=4)
    )
    orbital_of = (row_start + jnp.arange(row_count, dtype=jnp.int32)) // domain
    selector = (orbital_of[:, None] == jnp.arange(orbitals, dtype=jnp.int32)[None, :]).astype(
        jnp.float32
    )
    partial_energy = jnp.einsum(
        "lskj,ki->lsij", weighted, selector, precision=lax.Precision.HIGHEST
    )
    pair_energy = lax.psum(partial_energy, "pair") / (domain * domain)
    return (amplitudes, pair_energy)


def on_device(half_ints, partners, domains, occ_energy, vir_energy):
    _, _, orbitals, domain = half_ints.shape
    fits = partners.shape[0] == 2 and domain == 128 and vir_energy.shape[0] % domain == 0
    fits &= lax.axis_size("pair") == lax.axis_size("aux") == orbitals == 4
    step = fast if fits and half_ints.shape[0] % 16 == 0 else general
    return step(half_ints, partners, domains, occ_energy, vir_energy)


def solution(mesh):
    return jax.shard_map(
        on_device,
        mesh=mesh,
        in_specs=(
            P(("frag", "aux", "pair"), None, None, None),
            P(("frag", "aux"), None),
            P("frag", None),
            P("frag", None),
            P("frag"),
        ),
        out_specs=(P(("frag", "aux"), None, "pair", None), P(("frag", "aux"), None, None, None)),
        check_vma=False,
    )
```

```python
import jax
import jax.numpy as jnp
from jax import lax
from jax.experimental import pallas as pl
from jax.experimental.pallas import tpu as pltpu
from jax.sharding import PartitionSpec as P

BF16, F16, F32 = jnp.bfloat16, jnp.float16, jnp.float32
VMEM = pl.BlockSpec(memory_space=pltpu.VMEM)
SMEM = pl.BlockSpec(memory_space=pltpu.SMEM)
ANY = pl.BlockSpec(memory_space=pl.ANY)
PARAMS = pltpu.CompilerParams(vmem_limit_bytes=8 * 2**20)
PEAK_ROWS = 16
GROUPS = ([[(0, 1)]], [[(1, 1), (0, 2), (1, 2)]])

def shape(*dims, dtype=F32):
    return jax.ShapeDtypeStruct(dims, dtype)


def call(kernel, name, **options):
    return pl.pallas_call(kernel, compiler_params=PARAMS, name=name, **options)


def after(value, *others):
    return lax.optimization_barrier((value, *others))[0]


def panel_at(depth, orbital, block):
    return pl.ds((orbital * 2 + block) * depth, depth)


def depth_of(one_set, orbitals):
    return (one_set.shape[0] - PEAK_ROWS) // (2 * orbitals)


def pack(raw, count):
    depth, blocks, orbitals, domain = raw.shape
    rows = blocks * orbitals
    group = rows // 2

    def kernel(raw_ref, *refs):
        outs, (narrow, wide, sems) = refs[:count], refs[count:]
        z = lax.axis_index("aux")
        copies = []
        for n in range(2):
            start = pl.multiple_of((lax.div(z, 2) ^ (1 - n)) * group, 16)
            part = raw_ref.at[:, pl.ds(start, group), :]
            copies.append(pltpu.make_async_copy(part, narrow.at[n], sems.at[n]))
            copies[-1].start()
        peak = jnp.zeros((PEAK_ROWS, domain), F32)
        for n, ks in enumerate(((2, 3), (0, 1))):
            copies[n].wait()
            values = narrow[n].astype(F32).reshape(depth * group, domain)
            wide[n] = values
            values = jnp.max(jnp.abs(values).reshape(-1, PEAK_ROWS, domain), axis=0)
            peak = jnp.maximum(peak, values)
            for k in ks:
                first = lax.rem(z ^ k, 2) * 2 * orbitals
                for r in range(2):
                    for i in range(orbitals):
                        at = pl.ds(first + r * orbitals + i, depth, stride=group)
                        outs[k][panel_at(depth, i, r), :] = wide[n, at, :].astype(BF16)
        for out in outs:
            out[2 * orbitals * depth :, :] = peak.astype(BF16)

    one_set = shape(2 * orbitals * depth + PEAK_ROWS, domain, dtype=BF16)
    return call(
        kernel,
        "pack",
        out_shape=[one_set] * count,
        in_specs=[pl.BlockSpec(memory_space=pltpu.HBM)],
        out_specs=[VMEM] * count,
        scratch_shapes=[
            pltpu.VMEM((2, depth, group, domain), BF16),
            pltpu.VMEM((2, depth * group, domain), F32),
            pltpu.SemaphoreType.DMA((2,)),
        ],
    )(pltpu.with_memory_space_constraint(raw.reshape(depth, rows, domain), pltpu.HBM))


def relay(own, rows):
    domain = own[0].shape[1]

    def kernel(*refs):
        own_refs, outs = refs[:4], refs[4:]
        for out, partner in zip(outs, (1, 3)):
            for k in (1, 2, 3):
                out[(k - 1) * rows : k * rows] = own_refs[k ^ partner][:rows]

    return call(
        kernel,
        "relay",
        out_shape=[shape(3 * rows, domain, dtype=BF16)] * 2,
        in_specs=[VMEM] * 4,
        out_specs=[VMEM] * 2,
    )(*own)


def product(left, right):
    return lax.dot_general(left, right, (((0,), (0,)), ((), ())), preferred_element_type=F32)


def left_rows(own_refs, depth, r, part=slice(0, 4)):
    p = lax.axis_index("pair")
    x, c = p // 2, lax.rem(p, 2)
    order = (2 * x + c, 2 * (1 - x) + c, 2 * x + 1 - c, 2 * (1 - x) + 1 - c)
    columns = [
        jnp.concatenate([ref[panel_at(depth, i, r), :] for ref in own_refs], axis=0) for i in order[part]
    ]
    return jnp.concatenate(columns, axis=1)


def store_sums(sums, at, *outs):
    domain = sums.shape[0] // 4
    for n, out in enumerate(outs):
        out[at] = sums[n * domain : (n + 1) * domain]


def own_right(own_refs, depth, r, orbitals):
    columns = [
        jnp.concatenate([ref[panel_at(depth, j, r), :] for ref in own_refs], axis=0)
        for j in range(orbitals)
    ]
    return jnp.concatenate(columns, axis=1)


def own_pairs(own, orbitals, given):
    count, domain = len(own), own[0].shape[1]
    depth = depth_of(own[0], orbitals)
    wide = orbitals * domain
    part = slice(2, 4) if given else slice(0, 2)

    def kernel(*refs):
        own_refs, outs = refs[:count], refs[count:]
        if given:
            give, peak = outs
            top = own_refs[0][-PEAK_ROWS:, :].astype(F32)
            for ref in own_refs[1:]:
                top = jnp.maximum(top, ref[-PEAK_ROWS:, :].astype(F32))
            top = jnp.maximum(top[:8], top[8:])
            peak[...] = jnp.concatenate([top] * orbitals, axis=1)
            for n in range(2):
                give[n, 2 * domain :] = peak[...]
            outs = (give.at[0], give.at[1])
        for r in range(2):
            left = left_rows(own_refs, depth, r, part)
            sums = product(left, own_right(own_refs, depth, r, orbitals))
            at = slice(r * domain, (r + 1) * domain)
            outs[0][at], outs[1][at] = sums[:domain], sums[domain:]

    kept = [shape(2 * domain, wide)] * 2
    return call(
        kernel,
        "own_give" if given else "own_keep",
        out_shape=[shape(2, 2 * domain + 8, wide), shape(8, wide)] if given else kept,
        in_specs=[VMEM] * count,
        out_specs=[VMEM] * 2,
    )(*own)


def turn(own, orbitals):
    count, domain = len(own), own[0].shape[1]
    depth = depth_of(own[0], orbitals)

    def kernel(*refs):
        for r in range(2):
            refs[-1][r] = left_rows(refs[:count], depth, r).T

    return call(
        kernel,
        "turn",
        out_shape=shape(2, orbitals * domain, count * depth, dtype=BF16),
        in_specs=[VMEM] * count,
        out_specs=VMEM,
    )(*own)


def near_pairs(partners, turned, own, here, sides, orbitals, groups):
    count, domain = len(own), own[0].shape[1]
    depth = depth_of(own[0], orbitals)
    rows, wide = 2 * orbitals * depth, orbitals * domain

    def kernel(partners_ref, turned_ref, *refs):
        own_refs, here_refs, side_refs = refs[:count], refs[count : count + 2], refs[count + 2 :][:2]
        outs = refs[count + 4 :]
        z = lax.axis_index("aux")

        def flag(value):
            return jnp.broadcast_to(value, (depth, domain))

        def panels(r, j, slot, w):
            from_first = flag(jnp.where(w > 3, 1, 0) != lax.rem(z, 2))
            is_own, is_second = flag((w == 2) | (w == 3)), flag(lax.rem(w, 2) == 1)

            def either(first, second, start):
                rows_at = slice(start, start + depth)
                return jnp.where(from_first, first[rows_at, :], second[rows_at, :])

            found = []
            for k in range(count):
                refs, start = (here_refs, 0) if k == 0 else (side_refs, (k - 1) * rows)
                start += 2 * j * depth
                if slot == 1:
                    panel = either(*refs, start + r * depth)
                else:
                    panel = jnp.where(is_second, either(*refs, start + depth), either(*refs, start))
                    mine = [own_refs[k][panel_at(depth, j, block), :] for block in range(2)]
                    panel = jnp.where(is_own, jnp.where(is_second, mine[1], mine[0]), panel)
                found.append(panel)
            return jnp.concatenate(found, axis=0)

        for n, tiles in enumerate(groups):
            for t, (r, slot) in enumerate(tiles):
                w = partners_ref[r : r + 1, slot : slot + 1] - 2 * z + 2
                right = jnp.concatenate([panels(r, j, slot, w) for j in range(orbitals)], axis=1)
                sums = jnp.dot(turned_ref[r], right, preferred_element_type=F32)
                at = slice(t * domain, (t + 1) * domain)
                store_sums(sums, at, *outs[4 * n : 4 * n + 4])

    shapes = []
    for tiles in groups:
        shapes += [shape(len(tiles) * domain, wide)] * 4
    return call(
        kernel,
        "near",
        out_shape=shapes,
        in_specs=[VMEM] * (count + 6),
        out_specs=[VMEM] * len(shapes),
    )(partners, turned, *own, *here, *sides)


def scale_down(peak, got, depth):
    def kernel(peak_ref, got_ref, top_ref, down_ref):
        top = jnp.maximum(peak_ref[...], got_ref[0, -8:])
        top_ref[...] = top
        top = jnp.maximum(jnp.max(top[:, :128], axis=(0, 1), keepdims=True), 1e-17)
        down_ref[...] = jnp.broadcast_to(32768.0 / (top * top * depth), down_ref.shape)

    return call(
        kernel,
        "scale_down",
        out_shape=[shape(*peak.shape)] * 2,
        in_specs=[VMEM] * 2,
        out_specs=[VMEM] * 2,
    )(peak, got)


def scale_up(top, depth):
    def kernel(top_ref, up_ref):
        top = jnp.maximum(jnp.max(top_ref[:, :128], axis=(0, 1), keepdims=True), 1e-17)
        up_ref[...] = jnp.broadcast_to((top * top * depth) * (1.0 / 32768.0), up_ref.shape)

    return call(
        kernel, "scale_up", out_shape=shape(*top.shape), in_specs=[VMEM], out_specs=VMEM
    )(top)


def amplitude_tiles(total_ref, row_ref, col_ref, amp, energy_ref, tiles, done):
    rows, wide = amp.shape[1:]
    for t, (r, slot) in enumerate(tiles):
        row = row_ref[r]
        for j in range(wide // rows):
            at = slice(j * rows, (j + 1) * rows)
            total = total_ref[t * rows : (t + 1) * rows, at]
            tile = total / (row + col_ref[r, slot, j : j + 1, :])
            amp[t, :, at] = tile
            energy_ref[t, j : j + 1, :] = jnp.sum(total * tile, axis=0, keepdims=True)
        done(t)


def finish(totals, row_vals, col_vals, tiles, before, out):
    rows, wide = out[2:]
    count = len(tiles)

    def kernel(total_ref, row_ref, col_ref, *refs):
        amp_ref, energy_ref, amp, sems = refs[-4:]
        copies = []

        def done(t):
            r, slot = tiles[t]
            copies.append(pltpu.make_async_copy(amp.at[t], amp_ref.at[r, slot], sems.at[t]))
            copies[-1].start()

        amplitude_tiles(total_ref, row_ref, col_ref, amp, energy_ref, tiles, done)
        for started in copies:
            started.wait()

    return call(
        kernel,
        "finish",
        out_shape=[shape(*out), shape(count, wide // rows, rows)],
        in_specs=[VMEM] * 3 + [ANY] * len(before),
        out_specs=[ANY, VMEM],
        input_output_aliases={3: 0} if before else {},
        scratch_shapes=[pltpu.VMEM((count, rows, wide), F32), pltpu.SemaphoreType.DMA((count,))],
    )(totals, row_vals, col_vals, *before)


def finish_last(totals, row_vals, col_vals, tiles, before, shares):
    orbitals, domain = col_vals.shape[2:]
    wide = orbitals * domain
    blocks, slots = col_vals.shape[:2]
    count = len(tiles)
    known = len(shares)

    def kernel(total_ref, row_ref, col_ref, *refs):
        share_refs, (amp_ref, out, energy) = refs[:known], refs[known:]
        amplitude_tiles(total_ref, row_ref, col_ref, amp_ref, energy, tiles, lambda t: None)
        p = lax.axis_index("pair")
        row = lax.broadcasted_iota(jnp.int32, (orbitals, orbitals), 0)
        column = lax.broadcasted_iota(jnp.int32, (orbitals, orbitals), 1)
        for ref, places in zip((*share_refs, energy), (*before, tiles)):
            for t, (r, slot) in enumerate(places):
                sums = jnp.sum(ref[t], axis=1, keepdims=True) * (1.0 / (domain * domain))
                value = jnp.zeros((orbitals, orbitals), F32)
                for j in range(orbitals):
                    value = jnp.where((row == p) & (column == j), sums[j : j + 1, :], value)
                out[r, slot] = value

    return call(
        kernel,
        "finish_last",
        out_shape=[shape(count, domain, wide), shape(blocks, slots, orbitals, orbitals)],
        in_specs=[VMEM] * (3 + known),
        out_specs=[VMEM] * 2,
        scratch_shapes=[pltpu.VMEM((count, orbitals, domain), F32)],
    )(totals, row_vals, col_vals, *shares)


def put(tiles_at, values, amps):
    def kernel(values_ref, _, amp_ref, sems):
        copies = []
        for t, (r, slot) in enumerate(tiles_at):
            copies.append(pltpu.make_async_copy(values_ref.at[t], amp_ref.at[r, slot], sems.at[t]))
            copies[-1].start()
        for started in copies:
            started.wait()

    return call(
        kernel,
        "put",
        out_shape=shape(*amps.shape),
        in_specs=[VMEM, ANY],
        out_specs=ANY,
        input_output_aliases={1: 0},
        scratch_shapes=[pltpu.SemaphoreType.DMA((len(tiles_at),))],
    )(values, amps)


def last(shares):
    def kernel(*refs):
        refs[4][...] = (refs[0][...] + refs[1][...]) + (refs[2][...] + refs[3][...])

    return call(
        kernel,
        "last",
        out_shape=shape(*shares[0].shape),
        in_specs=[VMEM] * 4,
        out_specs=VMEM,
    )(*shares)


def energies(partners, domains, occ_energy, vir_energy):
    blocks, domain = domains.shape
    orbitals = occ_energy.shape[1]
    here, slots = partners.shape
    tables = vir_energy.shape[0] // domain

    def kernel(partners_ref, occ_ref, domains_ref, vir_ref, row_ref, col_ref, picked):
        at = domains_ref[...]
        lane, table = lax.rem(at, domain), lax.div(at, domain)
        vir = jnp.zeros(at.shape, F32)
        for t in range(tables):
            values = jnp.broadcast_to(vir_ref[t : t + 1, :], at.shape)
            vir = jnp.where(table == t, jnp.take_along_axis(values, lane, axis=1), vir)
        picked[...] = vir
        z, p = lax.axis_index("aux"), lax.axis_index("pair")
        for r in range(here):
            block = here * z + r
            value = occ_ref[p, block] - picked[pl.ds(block, 1), :]
            row_ref[r] = jnp.broadcast_to(value, (domain, domain)).T
            for s in range(slots):
                other = partners_ref[r, s]
                value = picked[pl.ds(other, 1), :]
                for j in range(orbitals):
                    col_ref[r, s, j : j + 1, :] = occ_ref[j, other] - value

    return call(
        kernel,
        "energies",
        out_shape=[shape(here, domain, domain), shape(here, slots, orbitals, domain)],
        in_specs=[SMEM] * 2 + [VMEM] * 2,
        out_specs=[VMEM] * 2,
        scratch_shapes=[pltpu.VMEM((blocks, domain), F32)],
    )(partners, occ_energy.T, domains, vir_energy.reshape(tables, domain))


def fast(half_ints, partners, domains, occ_energy, vir_energy):
    depth, _, orbitals, domain = half_ints.shape
    count = lax.axis_size("aux")
    wide = orbitals * domain
    sides = [[(i, i ^ 4) for i in range(16)], [(i, i ^ (12 if 4 <= i < 12 else 1)) for i in range(16)]]
    swap, cross, both = ([(i, i ^ k) for i in range(4)] for k in (1, 2, 3))

    own_here, *sends = pack(half_ints, count)
    here = [sends[0], sends[2]]
    own = [own_here]
    for k, send in enumerate(sends, 1):
        own.append(lax.ppermute(send, "aux", [(i, i ^ k) for i in range(count)]))
    row_vals, col_vals = energies(partners, domains, occ_energy, vir_energy)
    messages = relay(own, 2 * orbitals * depth)
    near = [lax.ppermute(m, ("aux", "pair"), side) for m, side in zip(messages, sides)]
    own[0] = after(own[0], *messages)

    def across(sums, axis_pairs):
        return lax.ppermute(sums, "pair", axis_pairs)

    give, peak = own_pairs(own, orbitals, True)
    mine, other = own_pairs(own, orbitals, False)
    got = across(give, swap)
    top, to_half = scale_down(peak, got, 2 * count * depth)
    half = ((other + got[1, : 2 * domain]) * to_half[:1]).astype(F16)
    parts = [(mine, got[0, : 2 * domain], across(half, cross))]
    from_half = scale_up(across(top, cross), 2 * count * depth)
    here[0] = after(here[0], parts[0][2], from_half, row_vals)

    groups = [[(0, 0), (1, 0)], *GROUPS[0], *GROUPS[1]]
    turned = turn(own, orbitals)
    sums = near_pairs(partners, turned, own, here, near, orbitals, GROUPS[0])
    here[0] = after(here[0], sums[0])
    sums += near_pairs(partners, turned, own, here, near, orbitals, GROUPS[1])
    mine_a, other_a, give_a, on_a, mine_b, other_b, give_b, on_b = sums
    half_a = ((other_a + across(on_a, swap)) * to_half[:1]).astype(F16)
    x_a = across(half_a, cross)
    on_b = after(on_b, half_a)
    half_b = ((other_b + across(on_b, swap)) * to_half[:1]).astype(F16)
    x_b = across(half_b, cross)
    parts.append((mine_a, across(after(give_a, half_a), swap), x_a))
    parts.append((mine_b, across(after(give_b, half_a), swap), x_b))

    out = partners.shape + (domain, wide)
    amps, shares = [], []
    for at, (mine, got, arrived) in enumerate(parts):
        back = after(from_half, shares[-1]) if at else from_half
        total = mine + got + arrived.astype(F32) * back[:1]
        if at < len(parts) - 1:
            *amps, share = finish(total, row_vals, col_vals, groups[at], amps, out)
            shares.append(share)
    values, share = finish_last(total, row_vals, col_vals, groups[-1], groups[:-1], shares)
    others = [lax.ppermute(share, "pair", to) for to in (swap, cross, both)]
    return put(groups[-1], values, amps[0]), last([share, *others])


def padded(shard, sides, width):
    for axis, dim in sides:
        size, length = (lax.axis_size(axis), shard.shape[dim])
        up = [(i, (i + 1) % size) for i in range(size - 1)]
        down = [(j, i) for i, j in up]
        last = lax.slice_in_dim(shard, length - width, length, axis=dim)
        first = lax.slice_in_dim(shard, 0, width, axis=dim)
        before = lax.ppermute(last, axis, up)
        after = lax.ppermute(first, axis, down)
        shard = jnp.concatenate([before, shard, after], axis=dim)
    return shard


def general(half_ints, partners, domains, occ_energy, vir_energy):
    blocks_here, slots = partners.shape
    orbitals = half_ints.shape[2]
    domain = half_ints.shape[3]
    row_width = orbitals * domain
    first_block = lax.axis_index("aux") * blocks_here
    owned = lax.all_to_all(half_ints, "aux", split_axis=1, concat_axis=0, tiled=True)
    widened = padded(owned, (("aux", 1),), blocks_here)
    flat_rows = widened.reshape(widened.shape[0], 3 * blocks_here, row_width)
    own_blocks = flat_rows[:, blocks_here : 2 * blocks_here]
    positions = (partners - first_block + blocks_here).reshape(-1)
    partner_rows = jnp.take(flat_rows, positions, axis=1).reshape(
        flat_rows.shape[0], blocks_here, slots, row_width
    )
    partial_terms = jnp.einsum(
        "qlr,qlsc->lsrc", own_blocks, partner_rows, preferred_element_type=jnp.float32
    )
    my_sums = lax.psum_scatter(partial_terms, "pair", scatter_dimension=2, tiled=True)
    row_count = my_sums.shape[2]
    row_start = lax.axis_index("pair") * row_count
    block_ids = first_block + jnp.arange(blocks_here, dtype=jnp.int32)
    row_vals = (
        jnp.take(occ_energy, block_ids, axis=0)[:, :, None]
        - jnp.take(vir_energy, jnp.take(domains, block_ids, axis=0), axis=0)[:, None, :]
    )
    row_vals = lax.dynamic_slice_in_dim(
        row_vals.reshape(blocks_here, row_width), row_start, row_count, 1
    )
    col_vals = (
        jnp.take(occ_energy, partners, axis=0)[:, :, :, None]
        - jnp.take(vir_energy, jnp.take(domains, partners, axis=0), axis=0)[:, :, None, :]
    )
    col_vals = col_vals.reshape(blocks_here, slots, row_width)
    denominator = row_vals[:, None, :, None] + col_vals[:, :, None, :]
    amplitudes = my_sums / denominator
    weighted = (
        (my_sums * amplitudes).reshape(blocks_here, slots, row_count, orbitals, domain).sum(axis=4)
    )
    orbital_of = (row_start + jnp.arange(row_count, dtype=jnp.int32)) // domain
    selector = (orbital_of[:, None] == jnp.arange(orbitals, dtype=jnp.int32)[None, :]).astype(
        jnp.float32
    )
    partial_energy = jnp.einsum(
        "lskj,ki->lsij", weighted, selector, precision=lax.Precision.HIGHEST
    )
    pair_energy = lax.psum(partial_energy, "pair") / (domain * domain)
    return (amplitudes, pair_energy)


def on_device(half_ints, partners, domains, occ_energy, vir_energy):
    _, _, orbitals, domain = half_ints.shape
    fits = partners.shape[0] == 2 and domain == 128 and vir_energy.shape[0] % domain == 0
    fits &= lax.axis_size("pair") == lax.axis_size("aux") == orbitals == 4
    step = fast if fits and half_ints.shape[0] % 16 == 0 else general
    return step(half_ints, partners, domains, occ_energy, vir_energy)


def solution(mesh):
    return jax.shard_map(
        on_device,
        mesh=mesh,
        in_specs=(
            P(("frag", "aux", "pair"), None, None, None),
            P(("frag", "aux"), None),
            P("frag", None),
            P("frag", None),
            P("frag"),
        ),
        out_specs=(P(("frag", "aux"), None, "pair", None), P(("frag", "aux"), None, None, None)),
        check_vma=False,
    )
```
